128 devices in a mesh: expert: 32 (over z, y, x_hi), replica: 2 (over core), group: 2 (over x_lo).
Axes of the slice: x: 4 (x_hi: 2, x_lo: 2; x = x_hi * 2 + x_lo), y: 4, z: 4, core: 2. Of those that a mesh axis runs over, the one named last changes fastest.
Arguments:
- tokens: bfloat16 [6144, 4096], P('expert', 'group'), may hold values from -6 to 6
- expert_ids: int32 [6144, 8], P('expert'), may hold values from 0 to 127, all different within a row; in each aligned block of 192 rows (0 to 191, 192 to 383, ...) at most 15 rows name the same one
- route_gates: float32 [6144, 8], P('expert'), may hold values from 0.03 to 0.5
- member_order: int32 [32], replicated, may hold values from 0 to 31, each once
- teach_gate: bfloat16 [32, 1536, 4096], P('expert', 'replica', 'group'), may hold values from -0.09375 to 0.09375
- teach_up: bfloat16 [32, 1536, 4096], P('expert', 'replica', 'group'), may hold values from -0.09375 to 0.09375
- teach_down: bfloat16 [32, 1536, 4096], P('expert', 'replica', 'group'), may hold values from -0.15625 to 0.15625
- stud_gate: bfloat16 [32, 1536, 2048], P('expert', 'replica', 'group'), may hold values from -0.09375 to 0.09375
- stud_up: bfloat16 [32, 1536, 2048], P('expert', 'replica', 'group'), may hold values from -0.09375 to 0.09375
- stud_down: bfloat16 [32, 1536, 2048], P('expert', 'replica', 'group'), may hold values from -0.15625 to 0.15625
Outputs:
- residual: float32 [6144, 4096], P('expert', ('group', 'replica'))
- grad_gate: bfloat16 [32, 1536, 2048], P('expert', 'replica', 'group')
- grad_up: bfloat16 [32, 1536, 2048], P('expert', 'replica', 'group')
- grad_down: bfloat16 [32, 1536, 2048], P('expert', 'replica', 'group')
The draws below stay inside these ranges and needn't reach their ends.
Inputs may be any that keep to these rules, and one draw needn't show every extreme that they name: `expert_ids`: each row names 8 different experts. Within each aligned block of 192 rows no expert is named by more than 15 rows. Only experts below 32 are in the window. `member_order`: every teacher expert of the window appears once.
All inputs are finite; a program needn't handle non-finite values.
Results may differ from the reference program's by a relative error of at most 0.025.
Values may be sent and summed in bfloat16 or wider, within the bound.
A program may use at most 128 MiB of HBM per device.

```python
import math
import jax
import jax.numpy as jnp
import numpy as np
from jax import lax

D = 4096
FF = 1536
EXPERTS = 128
TOPK = 8
TOK_DEV = 192
CAP = 15
TOKENS = 6144
TEACH = 32
STUD = 16
SUB = 512
N_EXPERT = 32
N_REPLICA = 2


def steps_of(own_key, dims, cuts, least, high):
    loudness, own = 1.0, jax.random.fold_in(own_key, 6)
    for dim, parts in cuts:
        steps = jnp.exp(jax.random.uniform(jax.random.fold_in(own, dim), (parts,), jnp.float32, least / len(cuts), high / len(cuts)))
        loudness = loudness * jnp.repeat(steps, dims[dim] // parts).reshape([-1 if axis == dim else 1 for axis in range(len(dims))])
    return loudness


def assign_block(rng, own, number, rows, count, top, limit, lean):
    sequence = jax.random.permutation(rng, count)
    packed, common = load_shares(count, rows * top, limit, lean, True), load_shares(count, rows * top, limit, lean, False)
    places = jnp.arange(count)

    def named(lengths, rotation):
        used = int((lengths > 0).sum())
        fixed = max(1, used // 4)
        moved = fixed + (places - fixed + rotation * (used - fixed)) % max(1, count - fixed)
        return jnp.zeros((count,), jnp.int32).at[sequence[jnp.where(places < fixed, places, moved)]].set(jnp.asarray(lengths, jnp.int32))

    lengths = jnp.where(number % 4 == 0, named(packed, number // 4), named(common, number - number // 4 - 1))
    mixed = jax.random.permutation(jax.random.fold_in(own, 3), count)
    source_of, taker = mixed[0:count // 2 * 2:2], mixed[1:count // 2 * 2:2]
    room = jnp.minimum(lengths[source_of] - 1, limit - lengths[taker]) // 2
    room = jnp.where((source_of == sequence[0]) | (taker == sequence[0]) | (lengths[taker] == 0), 0, jnp.maximum(room, 0))
    moved = jax.random.randint(jax.random.fold_in(own, 4), (count // 2,), 0, 1 << 20) % (room + 1)
    lengths = lengths.at[source_of].add(-moved).at[taker].add(moved)
    members = jnp.searchsorted(jnp.cumsum(lengths), jnp.arange(rows * top), side="right").astype(jnp.int32)
    grid = members.reshape(top, rows).T
    grid = grid[jax.random.permutation(jax.random.fold_in(own, 1), rows)]
    rotation = jax.random.randint(jax.random.fold_in(own, 2), (rows, 1), 0, top)
    return jnp.take_along_axis(grid, (jnp.arange(top)[None, :] + rotation) % top, axis=1)


def load_shares(amount, total, bound, skew, full):
    loads = [(1 << 20) // math.isqrt(grade ** skew) + 1 for grade in range(1, amount + 1)]
    largest = bound if full else min(bound, max(-(-total // amount), total * loads[0] // sum(loads)))
    least = 1 if total - largest >= amount - 1 else 0
    given, surplus = [largest] + [least] * (amount - 1), total - largest - least * (amount - 1)
    while surplus > 0:
        movable = [i for i in range(1, amount) if given[i] < largest] or [i for i in range(1, amount) if given[i] < bound]
        whole, remaining = sum([loads[i] for i in movable]), surplus
        for i in movable:
            addition = min(bound - given[i], max(1, remaining * loads[i] // whole), surplus)
            given[i] = given[i] + addition
            surplus = surplus - addition
    return np.array(given)


def normal_values(key, shape, scale, bound, shards=(), held_as=jnp.bfloat16):
    drawn = jax.random.normal(key, shape, jnp.float32) * scale
    if len(shards) > 0:
        drawn = steps_of(key, shape, shards, -0.22, 0.18) * drawn
    return jnp.clip(drawn, min=-bound, max=bound).astype(held_as)


def setup_inputs(seed: int = 0) -> dict:
    arg_keys = jax.random.split(jax.random.key(seed), 11)
    tokens = normal_values(arg_keys[0], (TOKENS, D), 1.0, 6.0, ((0, 32), (1, 2)))
    expert_ids_keys = jax.random.split(jax.random.fold_in(arg_keys[1], 1), TOKENS // TOK_DEV)
    expert_ids_turns = jax.random.permutation(jax.random.fold_in(arg_keys[1], 3), TOKENS // TOK_DEV)
    expert_ids = jax.vmap(lambda own, number: assign_block(jax.random.fold_in(arg_keys[1], 2), own, number, TOK_DEV, EXPERTS, TOPK, CAP, 2))(expert_ids_keys, expert_ids_turns).reshape((TOKENS, TOPK))
    route_gates = jnp.clip(jnp.exp(math.log(0.5) - 2.8134107 * jax.random.uniform(arg_keys[2], (TOKENS, TOPK), jnp.float32) ** steps_of(arg_keys[2], (TOKENS, TOPK), ((0, 32),), -0.2, 0.2)), 0.03, 0.5)
    member_order = jax.random.permutation(arg_keys[3], TEACH).astype(jnp.int32)
    teach_gate = normal_values(arg_keys[4], (TEACH, FF, D), D ** -0.5, 0.09375, ((0, 32), (1, 2), (2, 2)))
    teach_up = normal_values(arg_keys[5], (TEACH, FF, D), D ** -0.5, 0.09375, ((0, 32), (1, 2), (2, 2)))
    teach_down = normal_values(arg_keys[6], (TEACH, FF, D), FF ** -0.5, 0.15625, ((0, 32), (1, 2), (2, 2)))
    stud_gate = normal_values(arg_keys[7], (2 * STUD, FF, D // 2), D ** -0.5, 0.09375, ((0, 32), (1, 2), (2, 2)))
    stud_up = normal_values(arg_keys[8], (2 * STUD, FF, D // 2), D ** -0.5, 0.09375, ((0, 32), (1, 2), (2, 2)))
    stud_down = normal_values(arg_keys[9], (2 * STUD, FF, D // 2), FF ** -0.5, 0.15625, ((0, 32), (1, 2), (2, 2)))
    return {"tokens": tokens, "expert_ids": expert_ids, "route_gates": route_gates, "member_order": member_order, "teach_gate": teach_gate, "teach_up": teach_up, "teach_down": teach_down, "stud_gate": stud_gate, "stud_up": stud_up, "stud_down": stud_down}


def expert_slots(flat_ids, expert, slot_limit):
    pair_count = flat_ids.shape[0]
    chosen = flat_ids == expert
    rank_rows = jnp.cumsum(chosen.astype(jnp.int32)) - 1
    target = jnp.where(chosen, rank_rows, slot_limit).astype(jnp.int32)
    slot_table = jnp.full((slot_limit,), pair_count, jnp.int32)
    return slot_table.at[target].set(jnp.arange(pair_count, dtype=jnp.int32), mode="drop")


def full_rows(pair_block):
    shaped = pair_block.reshape(2, 2, N_REPLICA, SUB, FF)
    return shaped.transpose(1, 2, 0, 3, 4).reshape(D, FF)


def pack_rows(matrix):
    shaped = matrix.reshape(2, N_REPLICA, 2, SUB, FF)
    return shaped.transpose(2, 0, 1, 3, 4).reshape(2, D // 2, FF)


def full_cols(pair_block):
    shaped = pair_block.reshape(2, FF, 2, N_REPLICA, SUB)
    return shaped.transpose(1, 2, 3, 0, 4).reshape(FF, D)


def pack_cols(matrix):
    shaped = matrix.reshape(FF, 2, N_REPLICA, 2, SUB)
    return shaped.transpose(3, 0, 1, 2, 4).reshape(2, FF, D // 2)


def expert_forward(picked, gate_w, up_w, down_w):
    gate_pre = jnp.dot(picked, gate_w, preferred_element_type=jnp.float32)
    up_pre = jnp.dot(picked, up_w, preferred_element_type=jnp.float32)
    hidden = (gate_pre * jax.nn.sigmoid(gate_pre) * up_pre).astype(jnp.bfloat16)
    pieces = hidden.reshape(hidden.shape[0], N_REPLICA, FF // N_REPLICA).astype(jnp.float32)
    blocks = down_w.reshape(N_REPLICA, FF // N_REPLICA, D).astype(jnp.float32)
    partials = jnp.einsum("lrf,rfd->lrd", pieces, blocks).astype(jnp.bfloat16)
    partials = lax.optimization_barrier(partials)
    return jnp.sum(partials.astype(jnp.float32), axis=1)


def reference(tokens, expert_ids, route_gates, member_order, teach_gate, teach_up, teach_down, stud_gate, stud_up, stud_down):
    slot_limit = N_EXPERT * CAP
    flat_ids = expert_ids.reshape(-1)
    flat_gates = route_gates.reshape(-1)
    pair_count = flat_ids.shape[0]

    def gather_rows(merged):
        member_one = member_order[2 * merged]
        member_two = member_order[2 * merged + 1]
        slot_table = jnp.concatenate([expert_slots(flat_ids, member_one, slot_limit), expert_slots(flat_ids, member_two, slot_limit)])
        filled = slot_table < pair_count
        clamped = jnp.minimum(slot_table, pair_count - 1).astype(jnp.int32)
        token_index = (clamped // TOPK).astype(jnp.int32)
        weights = jnp.where(filled, flat_gates[clamped], jnp.zeros((), jnp.float32))
        picked = jnp.where(filled[:, None], tokens[token_index], jnp.zeros((), jnp.bfloat16))
        return member_one, member_two, token_index, weights, picked

    def merged_weights(merged):
        gate_w = full_rows(lax.dynamic_slice_in_dim(stud_gate, 2 * merged, 2, 0).transpose(0, 2, 1))
        up_w = full_rows(lax.dynamic_slice_in_dim(stud_up, 2 * merged, 2, 0).transpose(0, 2, 1))
        down_w = full_cols(lax.dynamic_slice_in_dim(stud_down, 2 * merged, 2, 0))
        return gate_w, up_w, down_w

    def forward_step(residual, merged):
        member_one, member_two, token_index, weights, picked = gather_rows(merged)
        teach_one = expert_forward(picked[:slot_limit], teach_gate[member_one].T, teach_up[member_one].T, teach_down[member_one])
        teach_two = expert_forward(picked[slot_limit:], teach_gate[member_two].T, teach_up[member_two].T, teach_down[member_two])
        teach_out = jnp.concatenate([teach_one, teach_two], axis=0)
        gate_w, up_w, down_w = merged_weights(merged)
        stud_out = expert_forward(picked, gate_w, up_w, down_w)
        term_rows = weights[:, None] * (stud_out - teach_out)
        return residual.at[token_index].add(term_rows), None

    residual, _ = lax.scan(forward_step, jnp.zeros((TOKENS, D), jnp.float32), jnp.arange(STUD, dtype=jnp.int32))

    def backward_step(merged):
        member_one, member_two, token_index, weights, picked = gather_rows(merged)
        gate_w, up_w, down_w = merged_weights(merged)
        gate_pre = jnp.dot(picked, gate_w, preferred_element_type=jnp.float32)
        up_pre = jnp.dot(picked, up_w, preferred_element_type=jnp.float32)
        sigmoid_gate = jax.nn.sigmoid(gate_pre)
        hidden = (gate_pre * sigmoid_gate * up_pre).astype(jnp.bfloat16)
        out_grad = (weights[:, None] * residual[token_index]).astype(jnp.bfloat16)
        back_hidden = lax.dot_general(out_grad, down_w, (((1,), (1,)), ((), ())), preferred_element_type=jnp.float32)
        gate_rows = (back_hidden * up_pre * sigmoid_gate * (1.0 + gate_pre * (1.0 - sigmoid_gate))).astype(jnp.bfloat16)
        up_rows = (back_hidden * gate_pre * sigmoid_gate).astype(jnp.bfloat16)
        inner = (((0,), (0,)), ((), ()))
        grad_gate = lax.dot_general(picked, gate_rows, inner, preferred_element_type=jnp.float32)
        grad_up = lax.dot_general(picked, up_rows, inner, preferred_element_type=jnp.float32)
        grad_down = lax.dot_general(hidden, out_grad, inner, preferred_element_type=jnp.float32)
        return (pack_rows(grad_gate).transpose(0, 2, 1).astype(jnp.bfloat16), pack_rows(grad_up).transpose(0, 2, 1).astype(jnp.bfloat16), pack_cols(grad_down).astype(jnp.bfloat16))

    gradients = lax.map(backward_step, jnp.arange(STUD, dtype=jnp.int32))
    grad_gate = gradients[0].reshape(2 * STUD, FF, D // 2)
    grad_up = gradients[1].reshape(2 * STUD, FF, D // 2)
    grad_down = gradients[2].reshape(2 * STUD, FF, D // 2)
    return (residual, grad_gate, grad_up, grad_down)
```

```python
import jax
import jax.numpy as jnp
from jax import lax
from jax.experimental import pallas as pl
from jax.experimental.pallas import tpu as pltpu
from jax.sharding import PartitionSpec as P

MESH = pl.DeviceIdType.MESH
BF = jnp.bfloat16
F32 = jnp.float32
OWNERS = 32
TOK = 192
SLOT = 16
TR = OWNERS * SLOT
SR = 2 * TR
HALF = SR // 4
HID = 768
COL = 1024
NAR = 512


def nn(a, b):
    return lax.dot_general(a, b, (((1,), (0,)), ((), ())), preferred_element_type=F32)


def nt(a, b):
    return lax.dot_general(a, b, (((1,), (1,)), ((), ())), preferred_element_type=F32)


def tn(a, b):
    return lax.dot_general(a, b, (((0,), (0,)), ((), ())), preferred_element_type=F32)


def hi_lo(v):
    hi = v.astype(BF)
    return hi, (v - hi.astype(F32)).astype(BF)


def body(
    ids,
    gates,
    order,
    tokens,
    tg,
    tu,
    td,
    sg,
    su,
    sd,
    res_o,
    gg_o,
    gu_o,
    gd_o,
    tok_v,
    tg_v,
    tu_v,
    td_v,
    sg_v,
    su_v,
    sd_v,
    t_onehot,
    s_onehot,
    comb,
    s_send,
    t_send,
    s_x,
    t_x,
    s_psend,
    s_pown,
    s_precv,
    t_psend,
    t_pown,
    t_precv,
    s_hid,
    t_hid,
    t_csend,
    t_crecv,
    t_ret,
    t_back,
    s_csend,
    s_crecv,
    s_ret,
    s_back,
    res_v,
    g_send,
    g_x,
    b_send,
    b_own,
    b_recv,
    gr_v,
    ur_v,
    load_sem,
    out_sem,
    a2a_s,
    a2a_r,
    core_s,
    core_r,
    ring_s,
    ring_r,
):
    me = lax.axis_index("expert")
    r = lax.axis_index("replica")
    g = lax.axis_index("group")
    h = lax.rem(me, 2)
    x = h * 2 + g
    pair = me - h
    nr = 1 - r

    def place(e):
        z, y, hh = e // 8, lax.rem(e // 2, 4), lax.rem(e, 2)
        return 8 * lax.rem(z + y, 4) + 2 * z + hh

    def peer(e):
        return {"expert": e, "replica": r, "group": g}

    def ring(p):
        return {"expert": pair + p // 2, "replica": r, "group": lax.rem(p, 2)}

    other_core = {"expert": me, "replica": nr, "group": g}
    partner = {"expert": me, "replica": r, "group": 1 - g}
    mine = place(me)

    def load(n, src, dst):
        return pltpu.make_async_copy(src, dst, load_sem.at[n])

    loads = [
        load(0, tokens.at[:, pl.ds(pl.multiple_of(r * COL, COL), COL)], tok_v),
        load(1, sg.at[0], sg_v),
        load(2, su.at[0], su_v),
        load(3, tg.at[0], tg_v),
        load(4, tu.at[0], tu_v),
        load(5, sd.at[0, :, pl.ds(0, NAR)], sd_v.at[0]),
        load(6, sd.at[0, :, pl.ds(NAR, NAR)], sd_v.at[1]),
        load(7, td.at[0, :, pl.ds(0, COL)], td_v.at[0]),
        load(8, td.at[0, :, pl.ds(COL, COL)], td_v.at[1]),
    ]
    for one in loads:
        one.start()

    barrier = pltpu.get_barrier_semaphore()

    @pl.loop(1, OWNERS)
    def _(k):
        pl.semaphore_signal(
            barrier, inc=1, device_id=peer(lax.rem(me + k, OWNERS)), device_id_type=MESH
        )

    pl.semaphore_signal(barrier, inc=1, device_id=other_core, device_id_type=MESH)
    pl.semaphore_signal(barrier, inc=1, device_id=partner, device_id_type=MESH)
    pl.semaphore_signal(barrier, inc=1, device_id=ring(lax.rem(3 - x, 4)), device_id_type=MESH)
    expert_col = lax.broadcasted_iota(jnp.int32, (TOK, OWNERS), 1)
    member = jnp.zeros((TOK, OWNERS), F32)
    gate = jnp.zeros((TOK, OWNERS), F32)
    for k in range(8):
        same = ids[:, k : k + 1] == expert_col
        member = jnp.where(same, 1.0, member)
        gate = jnp.where(same, gates[:, k : k + 1], gate)
    member_b = member.astype(BF)
    upto = (
        lax.broadcasted_iota(jnp.int32, (TOK, TOK), 1)
        <= lax.broadcasted_iota(jnp.int32, (TOK, TOK), 0)
    ).astype(F32).astype(BF)
    rank = (member * nn(upto, member_b)).astype(BF)
    slot_expert = lax.broadcasted_iota(jnp.int32, (OWNERS, TR), 1) // SLOT
    spread = (slot_expert == lax.broadcasted_iota(jnp.int32, (OWNERS, TR), 0)).astype(F32).astype(BF)
    turn = (lax.broadcasted_iota(jnp.int32, (OWNERS, OWNERS), 0) == order[0:1, :]).astype(F32).astype(BF)
    s_spread = nn(turn, spread).astype(BF)
    want = (lax.rem(lax.broadcasted_iota(jnp.int32, (TOK, TR), 1), SLOT) + 1).astype(F32)
    gate_hi, gate_lo = hi_lo(gate)
    s_hit = nn(rank, s_spread) == want
    t_hit = nn(rank, spread) == want
    s_onehot[...] = jnp.where(s_hit, 1.0, 0.0).astype(BF)
    t_onehot[...] = jnp.where(t_hit, 1.0, 0.0).astype(BF)
    comb[0] = jnp.where(s_hit, nn(gate_hi, s_spread), 0.0).astype(BF)
    comb[1] = jnp.where(s_hit, nn(gate_lo, s_spread), 0.0).astype(BF)
    comb[2] = jnp.where(t_hit, -nn(gate_hi, spread), 0.0).astype(BF)
    comb[3] = jnp.where(t_hit, -nn(gate_lo, spread), 0.0).astype(BF)
    loads[0].wait()
    for part in range(2):
        for hh in range(2):
            s_send[hh, part * 256 : (part + 1) * 256, :] = tn(
                s_onehot[:, part * 256 : (part + 1) * 256], tok_v[:, hh * NAR : (hh + 1) * NAR]
            ).astype(BF)
    pl.semaphore_wait(barrier, OWNERS + 2)

    def scatter(n, src_of, dst):
        @pl.loop(1, OWNERS)
        def _(k):
            e = lax.rem(me + k, OWNERS)
            pltpu.make_async_remote_copy(
                src_ref=src_of(e),
                dst_ref=dst,
                send_sem=a2a_s.at[n],
                recv_sem=a2a_r.at[n],
                device_id=peer(e),
                device_id_type=MESH,
            ).start()

    def all_sent(n, like):
        pltpu.make_async_copy(like, like, a2a_s.at[n]).wait()

    def all_here(n, like):
        pltpu.make_async_copy(like, like, a2a_r.at[n]).wait()

    def rows(e, size):
        return pl.ds(pl.multiple_of(e * size, size), size)

    s_rows, t_rows = rows(mine, 2 * SLOT), rows(mine, SLOT)
    m_rows = rows(me // 2, 2 * SLOT)
    scatter(0, lambda e: s_send.at[lax.rem(e, 2), rows(e // 2, 2 * SLOT)], s_x.at[r, s_rows])
    s_x[r, s_rows, :] = s_send[h, m_rows, :]
    for part in range(2):
        t_send[part * 256 : (part + 1) * 256, :] = tn(
            t_onehot[:, part * 256 : (part + 1) * 256], tok_v[...]
        ).astype(BF)
    scatter(1, lambda e: t_send.at[rows(e, SLOT)], t_x.at[r, t_rows])
    t_x[r, t_rows, :] = t_send[rows(me, SLOT), :]

    def to_core(n, src, dst):
        return pltpu.make_async_remote_copy(
            src_ref=src,
            dst_ref=dst,
            send_sem=core_s.at[n],
            recv_sem=core_r.at[n],
            device_id=other_core,
            device_id_type=MESH,
        )

    def to_ring(n, src, dst, p):
        return pltpu.make_async_remote_copy(
            src_ref=src,
            dst_ref=dst,
            send_sem=ring_s.at[n],
            recv_sem=ring_r.at[n],
            device_id=ring(p),
            device_id_type=MESH,
        )

    pending = []

    def go(copy):
        copy.start()
        pending.append(copy)
        return copy

    hops = (2, 1, 3, 0)
    shares = [lax.rem(x + d, 4) for d in hops]
    all_here(0, s_x.at[0, pl.ds(0, SR - 2 * SLOT)])
    swaps = []
    for i, q in enumerate(shares):
        block = rows(q, HALF)
        swaps.append(go(to_core(i, s_x.at[r, block], s_x.at[r, block])))
    loads[1].wait()
    loads[2].wait()

    s_pres = []
    for i, (d, q) in enumerate(zip(hops, shares)):
        swaps[i].wait_recv()
        block = rows(q, HALF)
        for n, w in enumerate((sg_v, su_v)):
            total = nt(s_x[0, block, :], w[:, :NAR]) + nt(s_x[1, block, :], w[:, NAR:])
            if d:
                s_psend[d - 1, n] = total.astype(BF)
            else:
                s_pown[n] = total
        if d:
            s_pres.append(go(to_ring(d - 1, s_psend.at[d - 1], s_precv.at[3 - d], q)))

    all_here(1, t_x.at[0, pl.ds(0, TR - SLOT)])
    t_swaps = []
    for i, half in enumerate((1 - g, g)):
        block = rows(half, HALF)
        t_swaps.append(go(to_core(4 + i, t_x.at[r, block], t_x.at[r, block])))
    loads[3].wait()
    loads[4].wait()
    for i, half in enumerate((1 - g, g)):
        t_swaps[i].wait_recv()
        block = rows(half, HALF)
        for n, w in enumerate((tg_v, tu_v)):
            total = nt(t_x[0, block, :], w[:, :COL]) + nt(t_x[1, block, :], w[:, COL:])
            if i == 0:
                t_psend[n] = total.astype(BF)
            else:
                t_pown[n] = total
        if i == 0:
            t_pre = go(
                pltpu.make_async_remote_copy(
                    src_ref=t_psend,
                    dst_ref=t_precv,
                    send_sem=ring_s.at[12],
                    recv_sem=ring_r.at[12],
                    device_id=partner,
                    device_id_type=MESH,
                )
            )
    t_pre.wait_recv()
    t_gate = t_pown[0] + t_precv[0].astype(F32)
    t_up = t_pown[1] + t_precv[1].astype(F32)
    own_half = rows(g, HALF)
    other_half = rows(1 - g, HALF)
    t_hid[own_half, :] = (t_gate * jax.nn.sigmoid(t_gate) * t_up).astype(BF)
    t_share = go(
        pltpu.make_async_remote_copy(
            src_ref=t_hid.at[own_half],
            dst_ref=t_hid.at[own_half],
            send_sem=ring_s.at[13],
            recv_sem=ring_r.at[13],
            device_id=partner,
            device_id_type=MESH,
        )
    )

    for one in s_pres:
        one.wait_recv()
    for n in range(2):
        s_pown[n] = (
            s_pown[n]
            + s_precv[0, n].astype(F32)
            + s_precv[1, n].astype(F32)
            + s_precv[2, n].astype(F32)
        )
    s_gate, s_up = s_pown[0], s_pown[1]
    own_share = rows(x, HALF)
    s_hid[own_share, :] = (s_gate * jax.nn.sigmoid(s_gate) * s_up).astype(BF)
    s_shares = []
    for d in (2, 1, 3):
        s_shares.append(
            go(to_ring(2 + d, s_hid.at[own_share], s_hid.at[own_share], lax.rem(x + d, 4)))
        )

    loads[7].wait()
    loads[8].wait()
    t_outs = []
    for i, block in enumerate((own_half, other_half)):
        if i == 1:
            t_share.wait_recv()
        t_csend[block, :] = nn(t_hid[block, :], td_v[nr]).astype(BF)
    t_out = go(to_core(6, t_csend, t_crecv))

    loads[5].wait()
    loads[6].wait()
    s_csend[own_share, :] = nn(s_hid[own_share, :], sd_v[nr]).astype(BF)

    t_out.wait_recv()
    for i in range(2):
        block = pl.ds(i * HALF, HALF)
        t_ret[block, :] = (nn(t_hid[block, :], td_v[r]) + t_crecv[block, :].astype(F32)).astype(BF)
    scatter(2, lambda e: t_ret.at[rows(place(e), SLOT)], t_back.at[rows(me, SLOT)])
    t_back[rows(me, SLOT), :] = t_ret[t_rows, :]

    for d, one in zip((2, 1, 3), s_shares):
        one.wait_recv()
        block = rows(lax.rem(x + 4 - d, 4), HALF)
        s_csend[block, :] = nn(s_hid[block, :], sd_v[nr]).astype(BF)
    s_out = go(to_core(7, s_csend, s_crecv))
    s_out.wait_recv()
    for i in range(4):
        block = pl.ds(i * HALF, HALF)
        s_ret[block, :] = (nn(s_hid[block, :], sd_v[r]) + s_crecv[block, :].astype(F32)).astype(BF)
    scatter(3, lambda e: s_ret.at[rows(place(e), 2 * SLOT)], s_back.at[h, m_rows])
    s_back[h, m_rows, :] = s_ret[s_rows, :]

    all_here(2, t_back.at[pl.ds(0, TR - SLOT)])
    all_here(3, s_x.at[0, pl.ds(0, SR - 2 * SLOT)])
    for hh in range(2):
        wide = slice(hh * NAR, (hh + 1) * NAR)
        back_s, back_t = s_back[hh], t_back[:, wide]
        residual = (
            nn(comb[0], back_s) + nn(comb[1], back_s) + nn(comb[2], back_t) + nn(comb[3], back_t)
        )
        res_v[:, wide] = residual
        res_hi, res_lo = hi_lo(residual)
        for part in range(2):
            tall = slice(part * 256, (part + 1) * 256)
            g_send[hh, tall, :] = (
                tn(comb[0, :, tall], res_hi)
                + tn(comb[0, :, tall], res_lo)
                + tn(comb[1, :, tall], res_hi)
            ).astype(BF)
    scatter(4, lambda e: g_send.at[lax.rem(e, 2), rows(e // 2, 2 * SLOT)], g_x.at[r, s_rows])
    g_x[r, s_rows, :] = g_send[h, m_rows, :]
    out_res = pltpu.make_async_copy(res_v, res_o, out_sem.at[0])
    out_res.start()

    all_here(4, g_x.at[0, pl.ds(0, SR - 2 * SLOT)])
    swaps = []
    for i, q in enumerate(shares):
        block = rows(q, HALF)
        swaps.append(go(to_core(8 + i, g_x.at[r, block], g_x.at[r, block])))
    b_sums = []
    for i, (d, q) in enumerate(zip(hops, shares)):
        swaps[i].wait_recv()
        block = rows(q, HALF)
        total = nt(g_x[0, block, :], sd_v[0]) + nt(g_x[1, block, :], sd_v[1])
        if d:
            b_send[d - 1] = total.astype(BF)
            b_sums.append(go(to_ring(5 + d, b_send.at[d - 1], b_recv.at[3 - d], q)))
        else:
            b_own[...] = total
    for b in range(2):
        for part in range(3):
            tall = slice(part * 256, (part + 1) * 256)
            td_v[0, tall, b * NAR : (b + 1) * NAR] = tn(s_hid[:, tall], g_x[b]).astype(BF)
    out_gd = pltpu.make_async_copy(td_v.at[0], gd_o.at[0], out_sem.at[1])
    out_gd.start()

    for one in b_sums:
        one.wait_recv()
    back = (
        b_own[...] + b_recv[0].astype(F32) + b_recv[1].astype(F32) + b_recv[2].astype(F32)
    )
    s_gate, s_up = s_pown[0], s_pown[1]
    sig = jax.nn.sigmoid(s_gate)
    gr_v[own_share, :] = (back * s_up * sig * (1.0 + s_gate * (1.0 - sig))).astype(BF)
    ur_v[own_share, :] = (back * s_gate * sig).astype(BF)
    row_shares = []
    for buf, n in ((gr_v, 14), (ur_v, 17)):
        for d in (2, 1, 3):
            row_shares.append(
                go(to_ring(n + d - 1, buf.at[own_share], buf.at[own_share], lax.rem(x + d, 4)))
            )

    for n, (buf, out) in enumerate(((gr_v, gg_o), (ur_v, gu_o))):
        for one in row_shares[3 * n : 3 * n + 3]:
            one.wait_recv()
        for b in range(2):
            for part in range(3):
                tall = slice(part * 256, (part + 1) * 256)
                target = td_v.at[1] if n == 0 else sg_v
                target[tall, b * NAR : (b + 1) * NAR] = tn(buf[:, tall], s_x[b]).astype(BF)
        done = pltpu.make_async_copy(td_v.at[1] if n == 0 else sg_v, out.at[0], out_sem.at[2 + n])
        done.start()
        if n == 0:
            out_gg = done
        else:
            out_gu = done

    all_sent(0, s_x.at[0, pl.ds(0, SR - 2 * SLOT)])
    all_sent(1, t_back.at[pl.ds(0, TR - SLOT)])
    all_sent(2, t_back.at[pl.ds(0, TR - SLOT)])
    all_sent(3, s_x.at[0, pl.ds(0, SR - 2 * SLOT)])
    all_sent(4, s_x.at[0, pl.ds(0, SR - 2 * SLOT)])
    for one in pending:
        one.wait_send()
    for one in (out_res, out_gd, out_gg, out_gu):
        one.wait()


def shards(tokens, ids, gates, order, tg, tu, td, sg, su, sd):
    vmem = pl.BlockSpec(memory_space=pltpu.VMEM)
    hbm = pl.BlockSpec(memory_space=pl.ANY)
    dma = pltpu.SemaphoreType.DMA

    def buf(*shape, dtype=BF):
        return pltpu.VMEM(shape, dtype)

    return pl.pallas_call(
        body,
        out_shape=(
            jax.ShapeDtypeStruct((TOK, COL), F32),
            jax.ShapeDtypeStruct((1, HID, COL), BF),
            jax.ShapeDtypeStruct((1, HID, COL), BF),
            jax.ShapeDtypeStruct((1, HID, COL), BF),
        ),
        in_specs=[vmem] * 3 + [hbm] * 7,
        out_specs=(hbm,) * 4,
        scratch_shapes=[
            buf(TOK, COL),
            buf(HID, 2 * COL),
            buf(HID, 2 * COL),
            buf(2, HID, COL),
            buf(HID, COL),
            buf(HID, COL),
            buf(2, HID, NAR),
            buf(TOK, TR),
            buf(TOK, TR),
            buf(4, TOK, TR),
            buf(2, TR, NAR),
            buf(TR, COL),
            buf(2, SR, NAR),
            buf(2, TR, COL),
            buf(3, 2, HALF, HID),
            buf(2, HALF, HID, dtype=F32),
            buf(3, 2, HALF, HID),
            buf(2, HALF, HID),
            buf(2, HALF, HID, dtype=F32),
            buf(2, HALF, HID),
            buf(SR, HID),
            buf(TR, HID),
            buf(TR, COL),
            buf(TR, COL),
            buf(TR, COL),
            buf(TR, COL),
            buf(SR, NAR),
            buf(SR, NAR),
            buf(SR, NAR),
            buf(2, TR, NAR),
            buf(TOK, COL, dtype=F32),
            buf(2, TR, NAR),
            buf(2, SR, NAR),
            buf(3, HALF, HID),
            buf(HALF, HID, dtype=F32),
            buf(3, HALF, HID),
            buf(SR, HID),
            buf(SR, HID),
            dma((9,)),
            dma((4,)),
            dma((5,)),
            dma((5,)),
            dma((12,)),
            dma((12,)),
            dma((20,)),
            dma((20,)),
        ],
        compiler_params=pltpu.CompilerParams(
            collective_id=0, has_side_effects=True, vmem_limit_bytes=60 << 20
        ),
        cost_estimate=pl.CostEstimate(
            flops=16_000_000_000, bytes_accessed=24_000_000, transcendentals=1_000_000
        ),
        name="distill",
    )(ids, gates, order.reshape(1, OWNERS), tokens, tg, tu, td, sg, su, sd)


def solution(mesh):
    weights = P("expert", "replica", "group")
    return jax.shard_map(
        shards,
        mesh=mesh,
        in_specs=(P("expert", "group"), P("expert", None), P("expert", None), P()) + (weights,) * 6,
        out_specs=(P("expert", ("group", "replica")), weights, weights, weights),
        check_vma=False,
    )
```

```python
import jax
import jax.numpy as jnp
from jax import lax
from jax.experimental import pallas as pl
from jax.experimental.pallas import tpu as pltpu
from jax.sharding import PartitionSpec as P

MESH = pl.DeviceIdType.MESH
BF = jnp.bfloat16
F32 = jnp.float32
OWNERS = 32
TOK = 192
SLOT = 16
TR = OWNERS * SLOT
SR = 2 * TR
HALF = SR // 4
HID = 768
COL = 1024
NAR = 512


def nn(a, b):
    return lax.dot_general(a, b, (((1,), (0,)), ((), ())), preferred_element_type=F32)


def nt(a, b):
    return lax.dot_general(a, b, (((1,), (1,)), ((), ())), preferred_element_type=F32)


def tn(a, b):
    return lax.dot_general(a, b, (((0,), (0,)), ((), ())), preferred_element_type=F32)


def hi_lo(v):
    hi = v.astype(BF)
    return hi, (v - hi.astype(F32)).astype(BF)


def body(
    ids,
    gates,
    order,
    tokens,
    tg,
    tu,
    td,
    sg,
    su,
    sd,
    res_o,
    gg_o,
    gu_o,
    gd_o,
    tok_v,
    tg_v,
    tu_v,
    td_v,
    sg_v,
    su_v,
    sd_v,
    t_onehot,
    s_onehot,
    comb,
    comb_t,
    s_send,
    t_send,
    s_x,
    t_x,
    s_psend,
    s_pown,
    s_pkeep,
    s_precv,
    t_psend,
    t_pown,
    t_precv,
    s_hid,
    t_hid,
    t_csend,
    t_crecv,
    t_ret,
    t_back,
    s_csend,
    s_crecv,
    s_ret,
    s_back,
    res_v,
    g_send,
    g_x,
    b_send,
    b_own,
    b_keep,
    b_recv,
    gr_v,
    ur_v,
    load_sem,
    out_sem,
    a2a_s,
    a2a_r,
    core_s,
    core_r,
    ring_s,
    ring_r,
):
    me = lax.axis_index("expert")
    r = lax.axis_index("replica")
    g = lax.axis_index("group")
    h = lax.rem(me, 2)
    x = h * 2 + g
    pair = me - h
    nr = 1 - r

    def place(e):
        z, y, hh = e // 8, lax.rem(e // 2, 4), lax.rem(e, 2)
        return 8 * lax.rem(z + y, 4) + 2 * z + hh

    def peer(e):
        return {"expert": e, "replica": r, "group": g}

    def ring(p):
        return {"expert": pair + p // 2, "replica": r, "group": lax.rem(p, 2)}

    right, left, opposite = lax.rem(x + 1, 4), lax.rem(x + 3, 4), lax.rem(x + 2, 4)
    near, across = h * 2 + 1 - g, 3 - x
    other_core = {"expert": me, "replica": nr, "group": g}
    partner = {"expert": me, "replica": r, "group": 1 - g}
    mine = place(me)

    def load(n, src, dst):
        return pltpu.make_async_copy(src, dst, load_sem.at[n])

    loads = [
        load(0, tokens.at[:, pl.ds(pl.multiple_of(r * COL, COL), COL)], tok_v),
        load(1, sg.at[0], sg_v),
        load(2, su.at[0], su_v),
        load(3, tg.at[0], tg_v),
        load(4, tu.at[0], tu_v),
        load(5, sd.at[0, :, pl.ds(0, NAR)], sd_v.at[0]),
        load(6, sd.at[0, :, pl.ds(NAR, NAR)], sd_v.at[1]),
        load(7, td.at[0, :, pl.ds(0, COL)], td_v.at[0]),
        load(8, td.at[0, :, pl.ds(COL, COL)], td_v.at[1]),
    ]
    for one in loads:
        one.start()

    barrier = pltpu.get_barrier_semaphore()

    @pl.loop(1, OWNERS)
    def _(k):
        pl.semaphore_signal(
            barrier, inc=1, device_id=peer(lax.rem(me + k, OWNERS)), device_id_type=MESH
        )

    pl.semaphore_signal(barrier, inc=1, device_id=other_core, device_id_type=MESH)
    pl.semaphore_signal(barrier, inc=1, device_id=partner, device_id_type=MESH)
    pl.semaphore_signal(barrier, inc=1, device_id=ring(across), device_id_type=MESH)
    expert_row = lax.broadcasted_iota(jnp.int32, (OWNERS, TOK), 0)
    member = jnp.zeros((OWNERS, TOK), F32)
    gate = jnp.zeros((OWNERS, TOK), F32)
    for k in range(8):
        same = ids[k : k + 1, :] == expert_row
        member = jnp.where(same, 1.0, member)
        gate = jnp.where(same, gates[k : k + 1, :], gate)
    upto = (
        lax.broadcasted_iota(jnp.int32, (TOK, TOK), 0)
        <= lax.broadcasted_iota(jnp.int32, (TOK, TOK), 1)
    ).astype(F32).astype(BF)
    rank = (member * nn(member.astype(BF), upto)).astype(BF)
    spread = (
        lax.broadcasted_iota(jnp.int32, (TR, OWNERS), 0) // SLOT
        == lax.broadcasted_iota(jnp.int32, (TR, OWNERS), 1)
    ).astype(F32).astype(BF)
    turn = (
        lax.broadcasted_iota(jnp.int32, (OWNERS, OWNERS), 0) == order[0:1, :]
    ).astype(F32).astype(BF)
    s_spread = nt(spread, turn).astype(BF)
    want = (lax.rem(lax.broadcasted_iota(jnp.int32, (TR, TOK), 0), SLOT) + 1).astype(F32)
    s_hit = nn(s_spread, rank) == want
    s_onehot[...] = jnp.where(s_hit, 1.0, 0.0).astype(BF)
    loads[0].wait()
    for hh in range(2):
        s_send[hh] = nn(s_onehot[...], tok_v[:, hh * NAR : (hh + 1) * NAR]).astype(BF)
    pl.semaphore_wait(barrier, OWNERS + 2)

    def scatter(n, src_of, dst):
        @pl.loop(1, OWNERS)
        def _(k):
            e = lax.rem(me + k, OWNERS)
            pltpu.make_async_remote_copy(
                src_ref=src_of(e),
                dst_ref=dst,
                send_sem=a2a_s.at[n],
                recv_sem=a2a_r.at[n],
                device_id=peer(e),
                device_id_type=MESH,
            ).start()

    def scatter_share(n, q, src_of, dst):
        @pl.loop(0, 8)
        def _(k):
            turned = lax.rem(k + me, 8)
            z = turned // 2
            e = 8 * z + 2 * lax.rem(q + 4 - z, 4) + lax.rem(turned, 2)

            @pl.when(e != me)
            def _():
                pltpu.make_async_remote_copy(
                    src_ref=src_of(e),
                    dst_ref=dst,
                    send_sem=a2a_s.at[n],
                    recv_sem=a2a_r.at[n],
                    device_id=peer(e),
                    device_id_type=MESH,
                ).start()

    def all_sent(n, like):
        pltpu.make_async_copy(like, like, a2a_s.at[n]).wait()

    def all_here(n, like):
        pltpu.make_async_copy(like, like, a2a_r.at[n]).wait()

    def rows(e, size):
        return pl.ds(pl.multiple_of(e * size, size), size)

    s_rows, t_rows = rows(mine, 2 * SLOT), rows(mine, SLOT)
    m_rows = rows(me // 2, 2 * SLOT)
    scatter(0, lambda e: s_send.at[lax.rem(e, 2), rows(e // 2, 2 * SLOT)], s_x.at[r, s_rows])
    s_x[r, s_rows, :] = s_send[h, m_rows, :]
    t_hit = nn(spread, rank) == want
    t_onehot[...] = jnp.where(t_hit, 1.0, 0.0).astype(BF)
    t_send[...] = nn(t_onehot[...], tok_v[...]).astype(BF)
    scatter(1, lambda e: t_send.at[rows(e, SLOT)], t_x.at[r, t_rows])
    t_x[r, t_rows, :] = t_send[rows(me, SLOT), :]
    gate_hi, gate_lo = hi_lo(gate)
    s_hit = s_onehot[...].astype(F32)
    t_hit = t_onehot[...].astype(F32)
    comb[0] = (s_hit * nn(s_spread, gate_hi)).astype(BF)
    comb[1] = (s_hit * nn(s_spread, gate_lo)).astype(BF)
    comb[2] = (t_hit * -nn(spread, gate_hi)).astype(BF)
    comb[3] = (t_hit * -nn(spread, gate_lo)).astype(BF)
    same_token = (
        lax.broadcasted_iota(jnp.int32, (TOK, TOK), 0)
        == lax.broadcasted_iota(jnp.int32, (TOK, TOK), 1)
    ).astype(F32).astype(BF)
    for n in range(4):
        comb_t[n] = nt(same_token, comb[n]).astype(BF)

    def to_core(n, src, dst):
        return pltpu.make_async_remote_copy(
            src_ref=src,
            dst_ref=dst,
            send_sem=core_s.at[n],
            recv_sem=core_r.at[n],
            device_id=other_core,
            device_id_type=MESH,
        )

    def to_ring(n, src, dst, p):
        return pltpu.make_async_remote_copy(
            src_ref=src,
            dst_ref=dst,
            send_sem=ring_s.at[n],
            recv_sem=ring_r.at[n],
            device_id=ring(p),
            device_id_type=MESH,
        )

    pending = []

    def go(copy):
        copy.start()
        pending.append(copy)
        return copy

    all_here(0, s_x.at[0, pl.ds(0, SR - 2 * SLOT)])
    order_of_shares = (opposite, across, near, x)
    swaps = []
    for i, q in enumerate(order_of_shares):
        block = rows(q, HALF)
        swaps.append(go(to_core(i, s_x.at[r, block], s_x.at[r, block])))
    loads[1].wait()
    loads[2].wait()
    across_sums = []
    for i, q in enumerate(order_of_shares):
        swaps[i].wait_recv()
        block = rows(q, HALF)
        for n, w in enumerate((sg_v, su_v)):
            total = nt(s_x[0, block, :], w[:, :NAR]) + nt(s_x[1, block, :], w[:, NAR:])
            if i < 2:
                s_psend[i, n] = total.astype(BF)
            elif i == 2:
                s_pkeep[n] = total
            else:
                s_pown[n] = total
        if i < 2:
            across_sums.append(go(to_ring(i, s_psend.at[i], s_precv.at[i], across)))

    all_here(1, t_x.at[0, pl.ds(0, TR - SLOT)])
    t_swaps = []
    for i, half in enumerate((1 - g, g)):
        block = rows(half, HALF)
        t_swaps.append(go(to_core(4 + i, t_x.at[r, block], t_x.at[r, block])))
    loads[3].wait()
    loads[4].wait()
    for i, half in enumerate((1 - g, g)):
        t_swaps[i].wait_recv()
        block = rows(half, HALF)
        for n, w in enumerate((tg_v, tu_v)):
            total = nt(t_x[0, block, :], w[:, :COL]) + nt(t_x[1, block, :], w[:, COL:])
            if i == 0:
                t_psend[n] = total.astype(BF)
            else:
                t_pown[n] = total
        if i == 0:
            t_pre = go(
                pltpu.make_async_remote_copy(
                    src_ref=t_psend,
                    dst_ref=t_precv,
                    send_sem=ring_s.at[12],
                    recv_sem=ring_r.at[12],
                    device_id=partner,
                    device_id_type=MESH,
                )
            )
    across_sums[0].wait_recv()
    for n in range(2):
        s_psend[2, n] = (s_pkeep[n] + s_precv[0, n].astype(F32)).astype(BF)
    near_sum = go(to_ring(2, s_psend.at[2], s_precv.at[2], near))
    t_pre.wait_recv()
    t_gate = t_pown[0] + t_precv[0].astype(F32)
    t_up = t_pown[1] + t_precv[1].astype(F32)
    own_half = rows(g, HALF)
    other_half = rows(1 - g, HALF)
    t_hid[own_half, :] = (t_gate * jax.nn.sigmoid(t_gate) * t_up).astype(BF)
    t_share = go(
        pltpu.make_async_remote_copy(
            src_ref=t_hid.at[own_half],
            dst_ref=t_hid.at[own_half],
            send_sem=ring_s.at[13],
            recv_sem=ring_r.at[13],
            device_id=partner,
            device_id_type=MESH,
        )
    )

    loads[7].wait()
    loads[8].wait()
    t_csend[own_half, :] = nn(t_hid[own_half, :], td_v[nr]).astype(BF)
    t_outs = [go(to_core(6, t_csend.at[own_half], t_crecv.at[own_half]))]

    def teacher_back(half, one):
        one.wait_recv()
        block = rows(half, HALF)
        t_ret[block, :] = (nn(t_hid[block, :], td_v[r]) + t_crecv[block, :].astype(F32)).astype(BF)
        for q in (2 * half, 2 * half + 1):
            scatter_share(2, q, lambda e: t_ret.at[rows(place(e), SLOT)], t_back.at[rows(me, SLOT)])

    across_sums[1].wait_recv()
    near_sum.wait_recv()
    for n in range(2):
        s_pown[n] = s_pown[n] + s_precv[1, n].astype(F32) + s_precv[2, n].astype(F32)
    s_gate, s_up = s_pown[0], s_pown[1]
    own_share = rows(x, HALF)
    s_hid[own_share, :] = (s_gate * jax.nn.sigmoid(s_gate) * s_up).astype(BF)
    own_hidden = s_hid.at[own_share]
    to_near = go(to_ring(3, own_hidden, own_hidden, near))
    to_across = go(to_ring(4, own_hidden, own_hidden, across))

    loads[5].wait()
    loads[6].wait()
    s_outs = []

    def merged_part(i, q):
        block = rows(q, HALF)
        s_csend[block, :] = nn(s_hid[block, :], sd_v[nr]).astype(BF)
        s_outs.append(go(to_core(8 + i, s_csend.at[block], s_crecv.at[block])))

    def merged_back(i, q):
        s_outs[i].wait_recv()
        block = rows(q, HALF)
        s_ret[block, :] = (nn(s_hid[block, :], sd_v[r]) + s_crecv[block, :].astype(F32)).astype(BF)
        scatter_share(
            3, q, lambda e: s_ret.at[rows(place(e), 2 * SLOT)], s_back.at[h, m_rows]
        )

    t_share.wait_recv()
    t_csend[other_half, :] = nn(t_hid[other_half, :], td_v[nr]).astype(BF)
    t_outs.append(go(to_core(7, t_csend.at[other_half], t_crecv.at[other_half])))
    merged_part(0, x)
    teacher_back(g, t_outs[0])
    teacher_back(1 - g, t_outs[1])
    t_back[rows(me, SLOT), :] = t_ret[t_rows, :]
    to_near.wait_recv()
    near_hidden = s_hid.at[rows(near, HALF)]
    passed_on = go(to_ring(5, near_hidden, near_hidden, across))
    merged_part(1, near)
    merged_back(0, x)
    to_across.wait_recv()
    merged_part(2, across)
    merged_back(1, near)
    merged_back(2, across)
    passed_on.wait_recv()
    merged_part(3, opposite)
    merged_back(3, opposite)
    s_back[h, m_rows, :] = s_ret[s_rows, :]

    all_here(2, t_back.at[pl.ds(0, TR - SLOT)])
    all_here(3, s_x.at[0, pl.ds(0, SR - 2 * SLOT)])
    for hh in range(2):
        wide = slice(hh * NAR, (hh + 1) * NAR)
        back_s, back_t = s_back[hh], t_back[:, wide]
        residual = (
            nn(comb_t[0], back_s)
            + nn(comb_t[1], back_s)
            + nn(comb_t[2], back_t)
            + nn(comb_t[3], back_t)
        )
        res_v[:, wide] = residual
        res_hi, res_lo = hi_lo(residual)
        g_send[hh] = (
            nn(comb[0], res_hi) + nn(comb[0], res_lo) + nn(comb[1], res_hi)
        ).astype(BF)
    scatter(4, lambda e: g_send.at[lax.rem(e, 2), rows(e // 2, 2 * SLOT)], g_x.at[r, s_rows])
    g_x[r, s_rows, :] = g_send[h, m_rows, :]
    out_res = pltpu.make_async_copy(res_v, res_o, out_sem.at[0])
    out_res.start()

    all_here(4, g_x.at[0, pl.ds(0, SR - 2 * SLOT)])
    order_of_shares = (opposite, right, left, x)
    swaps = []
    for i, q in enumerate(order_of_shares):
        block = rows(q, HALF)
        swaps.append(go(to_core(12 + i, g_x.at[r, block], g_x.at[r, block])))
    top, low = pl.ds(0, HALF // 2), pl.ds(HALF // 2, HALF // 2)
    for i, q in enumerate(order_of_shares):
        swaps[i].wait_recv()
        block = rows(q, HALF)
        total = nt(g_x[0, block, :], sd_v[0]) + nt(g_x[1, block, :], sd_v[1])
        if i == 0:
            b_send[0] = total.astype(BF)
            from_left = go(to_ring(6, b_send.at[0, top], b_recv.at[0, top], right))
            from_right = go(to_ring(7, b_send.at[0, low], b_recv.at[0, low], left))
        elif i == 1:
            b_send[1, low, :] = total[HALF // 2 :].astype(BF)
            b_keep[top, :] = total[: HALF // 2]
            left_low = go(to_ring(8, b_send.at[1, low], b_recv.at[1, low], right))
        elif i == 2:
            b_send[2, top, :] = total[: HALF // 2].astype(BF)
            b_keep[low, :] = total[HALF // 2 :]
            right_top = go(to_ring(9, b_send.at[2, top], b_recv.at[2, top], left))
        else:
            b_own[...] = total

    def down_grad(b):
        for part in range(3):
            tall = slice(part * 256, (part + 1) * 256)
            td_v[0, tall, b * NAR : (b + 1) * NAR] = tn(s_hid[:, tall], g_x[b]).astype(BF)

    down_grad(0)
    from_left.wait_recv()
    b_send[1, top, :] = (b_keep[top, :] + b_recv[0, top, :].astype(F32)).astype(BF)
    left_top = go(to_ring(10, b_send.at[1, top], b_recv.at[1, top], right))
    from_right.wait_recv()
    b_send[2, low, :] = (b_keep[low, :] + b_recv[0, low, :].astype(F32)).astype(BF)
    right_low = go(to_ring(11, b_send.at[2, low], b_recv.at[2, low], left))
    down_grad(1)
    out_gd = pltpu.make_async_copy(td_v.at[0], gd_o.at[0], out_sem.at[1])
    out_gd.start()

    for one in (left_low, right_top, left_top, right_low):
        one.wait_recv()
    back = b_own[...] + b_recv[1].astype(F32) + b_recv[2].astype(F32)
    s_gate, s_up = s_pown[0], s_pown[1]
    sig = jax.nn.sigmoid(s_gate)

    def part_of(q, lower):
        return pl.ds(pl.multiple_of(q * HALF + lower * (HALF // 2), HALF // 2), HALF // 2)

    def share_rows(n, buf):
        def send(i, q, lower, p):
            block = buf.at[part_of(q, lower)]
            return go(to_ring(n + i, block, block, p))

        return send, [send(0, x, 0, right), send(1, x, 1, left)], [
            send(2, x, 1, right),
            send(3, x, 0, left),
        ]

    def pass_rows(send, first):
        first[0].wait_recv()
        one = send(4, left, 0, right)
        first[1].wait_recv()
        return [one, send(5, right, 1, left)]

    gr_v[own_share, :] = (back * s_up * sig * (1.0 + s_gate * (1.0 - sig))).astype(BF)
    g_sender, g_first, g_rest = share_rows(14, gr_v)
    ur_v[own_share, :] = (back * s_gate * sig).astype(BF)
    g_rest = g_rest + pass_rows(g_sender, g_first)
    u_sender, u_first, u_rest = share_rows(20, ur_v)
    for one in g_rest:
        one.wait_recv()

    def weight_grad(buf, target, out, n):
        for b in range(2):
            for part in range(3):
                tall = slice(part * 256, (part + 1) * 256)
                target[tall, b * NAR : (b + 1) * NAR] = tn(buf[:, tall], s_x[b]).astype(BF)
        done = pltpu.make_async_copy(target, out.at[0], out_sem.at[n])
        done.start()
        return done

    u_rest = u_rest + pass_rows(u_sender, u_first)
    out_gg = weight_grad(gr_v, td_v.at[1], gg_o, 2)
    for one in u_rest:
        one.wait_recv()
    out_gu = weight_grad(ur_v, sg_v, gu_o, 3)

    all_sent(0, s_x.at[0, pl.ds(0, SR - 2 * SLOT)])
    all_sent(1, t_back.at[pl.ds(0, TR - SLOT)])
    all_sent(2, t_back.at[pl.ds(0, TR - SLOT)])
    all_sent(3, s_x.at[0, pl.ds(0, SR - 2 * SLOT)])
    all_sent(4, s_x.at[0, pl.ds(0, SR - 2 * SLOT)])
    for one in pending:
        one.wait_send()
    for one in (out_res, out_gd, out_gg, out_gu):
        one.wait()


def shards(tokens, ids, gates, order, tg, tu, td, sg, su, sd):
    vmem = pl.BlockSpec(memory_space=pltpu.VMEM)
    hbm = pl.BlockSpec(memory_space=pl.ANY)
    dma = pltpu.SemaphoreType.DMA

    def buf(*shape, dtype=BF):
        return pltpu.VMEM(shape, dtype)

    return pl.pallas_call(
        body,
        out_shape=(
            jax.ShapeDtypeStruct((TOK, COL), F32),
            jax.ShapeDtypeStruct((1, HID, COL), BF),
            jax.ShapeDtypeStruct((1, HID, COL), BF),
            jax.ShapeDtypeStruct((1, HID, COL), BF),
        ),
        in_specs=[vmem] * 3 + [hbm] * 7,
        out_specs=(hbm,) * 4,
        scratch_shapes=[
            buf(TOK, COL),
            buf(HID, 2 * COL),
            buf(HID, 2 * COL),
            buf(2, HID, COL),
            buf(HID, COL),
            buf(HID, COL),
            buf(2, HID, NAR),
            buf(TR, TOK),
            buf(TR, TOK),
            buf(4, TR, TOK),
            buf(4, TOK, TR),
            buf(2, TR, NAR),
            buf(TR, COL),
            buf(2, SR, NAR),
            buf(2, TR, COL),
            buf(3, 2, HALF, HID),
            buf(2, HALF, HID, dtype=F32),
            buf(2, HALF, HID, dtype=F32),
            buf(3, 2, HALF, HID),
            buf(2, HALF, HID),
            buf(2, HALF, HID, dtype=F32),
            buf(2, HALF, HID),
            buf(SR, HID),
            buf(TR, HID),
            buf(TR, COL),
            buf(TR, COL),
            buf(TR, COL),
            buf(TR, COL),
            buf(SR, NAR),
            buf(SR, NAR),
            buf(SR, NAR),
            buf(2, TR, NAR),
            buf(TOK, COL, dtype=F32),
            buf(2, TR, NAR),
            buf(2, SR, NAR),
            buf(3, HALF, HID),
            buf(HALF, HID, dtype=F32),
            buf(HALF, HID, dtype=F32),
            buf(3, HALF, HID),
            buf(SR, HID),
            buf(SR, HID),
            dma((9,)),
            dma((4,)),
            dma((5,)),
            dma((5,)),
            dma((16,)),
            dma((16,)),
            dma((26,)),
            dma((26,)),
        ],
        compiler_params=pltpu.CompilerParams(
            collective_id=0, has_side_effects=True, vmem_limit_bytes=60 << 20
        ),
        cost_estimate=pl.CostEstimate(
            flops=16_000_000_000, bytes_accessed=24_000_000, transcendentals=1_000_000
        ),
        name="distill",
    )(ids.T, gates.T, order.reshape(1, OWNERS), tokens, tg, tu, td, sg, su, sd)


def solution(mesh):
    weights = P("expert", "replica", "group")
    return jax.shard_map(
        shards,
        mesh=mesh,
        in_specs=(P("expert", "group"), P("expert", None), P("expert", None), P()) + (weights,) * 6,
        out_specs=(P("expert", ("group", "replica")), weights, weights, weights),
        check_vma=False,
    )
```

```python
import jax
import jax.numpy as jnp
from jax import lax
from jax.experimental import pallas as pl
from jax.experimental.pallas import tpu as pltpu
from jax.sharding import PartitionSpec as P

MESH = pl.DeviceIdType.MESH
BF = jnp.bfloat16
F32 = jnp.float32
OWNERS = 32
TOK = 192
SLOT = 16
TR = OWNERS * SLOT
SR = 2 * TR
HALF = SR // 4
PACK = HALF // SLOT * (SLOT - 1)
HID = 768
COL = 1024
NAR = 512


def nn(a, b):
    return lax.dot_general(a, b, (((1,), (0,)), ((), ())), preferred_element_type=F32)


def nt(a, b):
    return lax.dot_general(a, b, (((1,), (1,)), ((), ())), preferred_element_type=F32)


def tn(a, b):
    return lax.dot_general(a, b, (((0,), (0,)), ((), ())), preferred_element_type=F32)


def hi_lo(v):
    hi = v.astype(BF)
    return hi, (v - hi.astype(F32)).astype(BF)


def body(
    ids,
    gates,
    order,
    tokens,
    tg,
    tu,
    td,
    sg,
    su,
    sd,
    res_o,
    gg_o,
    gd_o,
    ur_o,
    sc_o,
    tok_v,
    tg_v,
    tu_v,
    td_v,
    sg_v,
    su_v,
    sd_v,
    t_onehot,
    s_onehot,
    comb,
    comb_t,
    s_send,
    t_send,
    s_x,
    s_c,
    t_x,
    pack,
    unpack,
    s_psend,
    s_pown,
    s_pkeep,
    s_precv,
    t_psend,
    t_pown,
    t_precv,
    s_hid,
    t_hid,
    t_csend,
    t_crecv,
    t_ret,
    t_back,
    s_csend,
    s_crecv,
    s_ret,
    s_back,
    res_v,
    g_send,
    g_x,
    g_c,
    b_send,
    b_own,
    b_keep,
    b_recv,
    gr_v,
    ur_v,
    load_sem,
    out_sem,
    a2a_s,
    a2a_r,
    core_s,
    core_r,
    ring_s,
    ring_r,
):
    me = lax.axis_index("expert")
    r = lax.axis_index("replica")
    g = lax.axis_index("group")
    h = lax.rem(me, 2)
    x = h * 2 + g
    pair = me - h
    nr = 1 - r

    def place(e):
        z, y, hh = e // 8, lax.rem(e // 2, 4), lax.rem(e, 2)
        return 8 * lax.rem(z + y, 4) + 2 * z + hh

    def peer(e):
        return {"expert": e, "replica": r, "group": g}

    def ring(p):
        return {"expert": pair + p // 2, "replica": r, "group": lax.rem(p, 2)}

    right, left, opposite = lax.rem(x + 1, 4), lax.rem(x + 3, 4), lax.rem(x + 2, 4)
    near, across = h * 2 + 1 - g, 3 - x
    other_core = {"expert": me, "replica": nr, "group": g}
    partner = {"expert": me, "replica": r, "group": 1 - g}
    mine = place(me)

    def load(n, src, dst):
        return pltpu.make_async_copy(src, dst, load_sem.at[n])

    loads = [
        load(0, tokens.at[:, pl.ds(pl.multiple_of(r * COL, COL), COL)], tok_v),
        load(1, sg.at[0], sg_v),
        load(2, su.at[0], su_v),
        load(3, tg.at[0], tg_v),
        load(4, tu.at[0], tu_v),
        load(5, sd.at[0, :, pl.ds(0, NAR)], sd_v.at[0]),
        load(6, sd.at[0, :, pl.ds(NAR, NAR)], sd_v.at[1]),
        load(7, td.at[0, :, pl.ds(0, COL)], td_v.at[0]),
        load(8, td.at[0, :, pl.ds(COL, COL)], td_v.at[1]),
    ]
    for one in loads:
        one.start()

    barrier = pltpu.get_barrier_semaphore()

    @pl.loop(1, OWNERS)
    def _(k):
        pl.semaphore_signal(
            barrier, inc=1, device_id=peer(lax.rem(me + k, OWNERS)), device_id_type=MESH
        )

    pl.semaphore_signal(barrier, inc=1, device_id=other_core, device_id_type=MESH)
    pl.semaphore_signal(barrier, inc=1, device_id=partner, device_id_type=MESH)
    pl.semaphore_signal(barrier, inc=1, device_id=ring(across), device_id_type=MESH)
    expert_row = lax.broadcasted_iota(jnp.int32, (OWNERS, TOK), 0)
    member = jnp.zeros((OWNERS, TOK), F32)
    gate = jnp.zeros((OWNERS, TOK), F32)
    for k in range(8):
        same = ids[k : k + 1, :] == expert_row
        member = jnp.where(same, 1.0, member)
        gate = jnp.where(same, gates[k : k + 1, :], gate)
    upto = (
        lax.broadcasted_iota(jnp.int32, (TOK, TOK), 0)
        <= lax.broadcasted_iota(jnp.int32, (TOK, TOK), 1)
    ).astype(F32).astype(BF)
    rank = (member * nn(member.astype(BF), upto)).astype(BF)
    spread = (
        lax.shift_right_logical(lax.broadcasted_iota(jnp.int32, (TR, OWNERS), 0), 4)
        == lax.broadcasted_iota(jnp.int32, (TR, OWNERS), 1)
    ).astype(F32).astype(BF)
    turn = (
        lax.broadcasted_iota(jnp.int32, (OWNERS, OWNERS), 0) == order[0:1, :]
    ).astype(F32).astype(BF)
    s_spread = nt(spread, turn).astype(BF)
    want = ((lax.broadcasted_iota(jnp.int32, (TR, 1), 0) & (SLOT - 1)) + 1).astype(F32)
    s_hit = nn(s_spread, rank) == want
    s_onehot[...] = jnp.where(s_hit, 1.0, 0.0).astype(BF)
    loads[0].wait()
    for hh in range(2):
        s_send[hh] = nn(s_onehot[...], tok_v[:, hh * NAR : (hh + 1) * NAR]).astype(BF)
    pl.semaphore_wait(barrier, OWNERS + 2)

    def scatter(n, src_of, dst):
        @pl.loop(1, OWNERS)
        def _(k):
            e = lax.rem(me + k, OWNERS)
            pltpu.make_async_remote_copy(
                src_ref=src_of(e),
                dst_ref=dst,
                send_sem=a2a_s.at[n],
                recv_sem=a2a_r.at[n],
                device_id=peer(e),
                device_id_type=MESH,
            ).start()

    def scatter_share(n, q, src_of, dst):
        @pl.loop(0, 8)
        def _(k):
            turned = lax.rem(k + me, 8)
            z = turned // 2
            e = 8 * z + 2 * lax.rem(q + 4 - z, 4) + lax.rem(turned, 2)

            @pl.when(e != me)
            def _():
                pltpu.make_async_remote_copy(
                    src_ref=src_of(e),
                    dst_ref=dst,
                    send_sem=a2a_s.at[n],
                    recv_sem=a2a_r.at[n],
                    device_id=peer(e),
                    device_id_type=MESH,
                ).start()

    def all_sent(n, like):
        pltpu.make_async_copy(like, like, a2a_s.at[n]).wait()

    def all_here(n, like):
        pltpu.make_async_copy(like, like, a2a_r.at[n]).wait()

    def rows(e, size):
        return pl.ds(pl.multiple_of(e * size, size), size)

    s_rows, t_rows = rows(mine, 2 * SLOT), rows(mine, SLOT)
    m_rows = rows(me // 2, 2 * SLOT)
    scatter(0, lambda e: s_send.at[lax.rem(e, 2), rows(e // 2, 2 * SLOT)], s_x.at[r, s_rows])
    s_x[r, s_rows, :] = s_send[h, m_rows, :]
    t_hit = nn(spread, rank) == want
    t_onehot[...] = jnp.where(t_hit, 1.0, 0.0).astype(BF)
    t_send[...] = nn(t_onehot[...], tok_v[...]).astype(BF)
    scatter(1, lambda e: t_send.at[rows(e, SLOT)], t_x.at[r, t_rows])
    t_x[r, t_rows, :] = t_send[rows(me, SLOT), :]
    gate_hi, gate_lo = hi_lo(gate)
    s_hit = s_onehot[...].astype(F32)
    t_hit = t_onehot[...].astype(F32)
    comb[0] = (s_hit * nn(s_spread, gate_hi)).astype(BF)
    comb[1] = (s_hit * nn(s_spread, gate_lo)).astype(BF)
    comb[2] = (t_hit * -nn(spread, gate_hi)).astype(BF)
    comb[3] = (t_hit * -nn(spread, gate_lo)).astype(BF)
    same_token = (
        lax.broadcasted_iota(jnp.int32, (TOK, TOK), 0)
        == lax.broadcasted_iota(jnp.int32, (TOK, TOK), 1)
    ).astype(F32).astype(BF)
    for n in range(4):
        comb_t[n] = nt(same_token, comb[n]).astype(BF)

    def packed_place(shape, dim):
        slot = lax.broadcasted_iota(jnp.int32, shape, dim)
        inner = slot & (SLOT - 1)
        to = lax.shift_right_logical(slot, 4) * (SLOT - 1) + inner
        hit = (to == lax.broadcasted_iota(jnp.int32, shape, 1 - dim)) & (inner < SLOT - 1)
        return jnp.where(hit, 1.0, 0.0).astype(BF)

    pack[...] = packed_place((PACK, HALF), 1)
    unpack[...] = packed_place((HALF, PACK), 0)

    def packed(block):
        return nn(pack[...], block).astype(BF)

    def unpacked(block):
        return nn(unpack[...], block).astype(BF)

    def to_core(n, src, dst):
        return pltpu.make_async_remote_copy(
            src_ref=src,
            dst_ref=dst,
            send_sem=core_s.at[n],
            recv_sem=core_r.at[n],
            device_id=other_core,
            device_id_type=MESH,
        )

    def to_ring(n, src, dst, p):
        return pltpu.make_async_remote_copy(
            src_ref=src,
            dst_ref=dst,
            send_sem=ring_s.at[n],
            recv_sem=ring_r.at[n],
            device_id=ring(p),
            device_id_type=MESH,
        )

    pending = []

    def go(copy):
        copy.start()
        pending.append(copy)
        return copy

    all_here(0, s_x.at[0, pl.ds(0, SR - 2 * SLOT)])
    order_of_shares = (opposite, across, near, x)
    swaps = []
    for i, q in enumerate(order_of_shares):
        block = rows(q, HALF)
        swaps.append(go(to_core(i, s_x.at[r, block], s_x.at[r, block])))
    loads[1].wait()
    loads[2].wait()
    for i, q in enumerate(order_of_shares):
        swaps[i].wait_recv()
        block, small = rows(q, HALF), rows(q, PACK)
        for b in range(2):
            s_c[b, small, :] = packed(s_x[b, block, :])
        for n, w in enumerate((sg_v, su_v)):
            total = nt(s_c[0, small, :], w[:, :NAR]) + nt(s_c[1, small, :], w[:, NAR:])
            if i < 2:
                s_psend[i, n] = total.astype(BF)
            elif i == 2:
                s_pkeep[n] = total
            else:
                s_pown[n] = total
        if i == 0:
            first_sum = go(to_ring(0, s_psend.at[0], s_precv.at[0], across))

    out_sc = pltpu.make_async_copy(s_c, sc_o, out_sem.at[3])
    out_sc.start()

    all_here(1, t_x.at[0, pl.ds(0, TR - SLOT)])
    t_swaps = []
    for i, half in enumerate((1 - g, g)):
        block = rows(half, HALF)
        t_swaps.append(go(to_core(4 + i, t_x.at[r, block], t_x.at[r, block])))
    loads[3].wait()
    loads[4].wait()
    for i, half in enumerate((1 - g, g)):
        t_swaps[i].wait_recv()
        block = rows(half, HALF)
        t_rows_a, t_rows_b = packed(t_x[0, block, :]), packed(t_x[1, block, :])
        for n, w in enumerate((tg_v, tu_v)):
            total = nt(t_rows_a, w[:, :COL]) + nt(t_rows_b, w[:, COL:])
            if i == 0:
                t_psend[n] = total.astype(BF)
            else:
                t_pown[n] = total
        if i == 0:
            t_pre = go(
                pltpu.make_async_remote_copy(
                    src_ref=t_psend,
                    dst_ref=t_precv,
                    send_sem=ring_s.at[12],
                    recv_sem=ring_r.at[12],
                    device_id=partner,
                    device_id_type=MESH,
                )
            )
    first_sum.wait_recv()
    across_sum = go(to_ring(1, s_psend.at[1], s_precv.at[1], across))
    for n in range(2):
        s_psend[2, n] = (s_pkeep[n] + s_precv[0, n].astype(F32)).astype(BF)
    near_sum = go(to_ring(2, s_psend.at[2], s_precv.at[2], near))
    t_pre.wait_recv()
    t_gate = t_pown[0] + t_precv[0].astype(F32)
    t_up = t_pown[1] + t_precv[1].astype(F32)
    own_half = rows(g, PACK)
    other_half = rows(1 - g, PACK)
    t_hid[own_half, :] = (t_gate * jax.nn.sigmoid(t_gate) * t_up).astype(BF)
    t_share = go(
        pltpu.make_async_remote_copy(
            src_ref=t_hid.at[own_half],
            dst_ref=t_hid.at[own_half],
            send_sem=ring_s.at[13],
            recv_sem=ring_r.at[13],
            device_id=partner,
            device_id_type=MESH,
        )
    )

    loads[7].wait()
    loads[8].wait()
    t_csend[own_half, :] = nn(t_hid[own_half, :], td_v[nr]).astype(BF)
    t_outs = [go(to_core(6, t_csend.at[own_half], t_crecv.at[own_half]))]

    def teacher_back(half, one):
        one.wait_recv()
        block = rows(half, PACK)
        total = nn(t_hid[block, :], td_v[r]) + t_crecv[block, :].astype(F32)
        t_ret[rows(half, HALF), :] = unpacked(total.astype(BF))
        for q in (2 * half, 2 * half + 1):
            scatter_share(2, q, lambda e: t_ret.at[rows(place(e), SLOT)], t_back.at[rows(me, SLOT)])

    across_sum.wait_recv()
    near_sum.wait_recv()
    for n in range(2):
        s_pown[n] = s_pown[n] + s_precv[1, n].astype(F32) + s_precv[2, n].astype(F32)
    s_gate, s_up = s_pown[0], s_pown[1]
    own_share = rows(x, PACK)
    s_hid[own_share, :] = (s_gate * jax.nn.sigmoid(s_gate) * s_up).astype(BF)
    own_hidden = s_hid.at[own_share]
    to_near = go(to_ring(3, own_hidden, own_hidden, near))
    to_across = go(to_ring(4, own_hidden, own_hidden, across))

    loads[5].wait()
    loads[6].wait()
    s_outs = []

    def merged_part(i, q):
        block = rows(q, PACK)
        s_csend[block, :] = nn(s_hid[block, :], sd_v[nr]).astype(BF)
        s_outs.append(go(to_core(8 + i, s_csend.at[block], s_crecv.at[block])))

    def merged_back(i, q):
        s_outs[i].wait_recv()
        block = rows(q, PACK)
        total = nn(s_hid[block, :], sd_v[r]) + s_crecv[block, :].astype(F32)
        s_ret[rows(q, HALF), :] = unpacked(total.astype(BF))
        scatter_share(
            3, q, lambda e: s_ret.at[rows(place(e), 2 * SLOT)], s_back.at[h, m_rows]
        )

    t_share.wait_recv()
    t_csend[other_half, :] = nn(t_hid[other_half, :], td_v[nr]).astype(BF)
    t_outs.append(go(to_core(7, t_csend.at[other_half], t_crecv.at[other_half])))
    merged_part(0, x)
    teacher_back(g, t_outs[0])
    teacher_back(1 - g, t_outs[1])
    t_back[rows(me, SLOT), :] = t_ret[t_rows, :]
    to_near.wait_recv()
    near_hidden = s_hid.at[rows(near, PACK)]
    passed_on = go(to_ring(5, near_hidden, near_hidden, across))
    merged_part(1, near)
    to_across.wait_recv()
    merged_part(2, across)
    passed_on.wait_recv()
    merged_part(3, opposite)
    merged_back(0, x)
    merged_back(1, near)
    merged_back(2, across)
    merged_back(3, opposite)
    s_back[h, m_rows, :] = s_ret[s_rows, :]

    all_here(2, t_back.at[pl.ds(0, TR - SLOT)])
    all_here(3, s_x.at[0, pl.ds(0, SR - 2 * SLOT)])
    for hh in range(2):
        wide = slice(hh * NAR, (hh + 1) * NAR)
        back_s, back_t = s_back[hh], t_back[:, wide]
        residual = (
            nn(comb_t[0], back_s)
            + nn(comb_t[1], back_s)
            + nn(comb_t[2], back_t)
            + nn(comb_t[3], back_t)
        )
        res_v[:, wide] = residual
        res_hi, res_lo = hi_lo(residual)
        g_send[hh] = (
            nn(comb[0], res_hi) + nn(comb[0], res_lo) + nn(comb[1], res_hi)
        ).astype(BF)
    scatter(4, lambda e: g_send.at[lax.rem(e, 2), rows(e // 2, 2 * SLOT)], g_x.at[r, s_rows])
    g_x[r, s_rows, :] = g_send[h, m_rows, :]
    out_res = pltpu.make_async_copy(res_v, res_o, out_sem.at[0])
    out_res.start()

    all_here(4, g_x.at[0, pl.ds(0, SR - 2 * SLOT)])
    order_of_shares = (opposite, right, left, x)
    swaps = []
    for i, q in enumerate(order_of_shares):
        block = rows(q, HALF)
        swaps.append(go(to_core(12 + i, g_x.at[r, block], g_x.at[r, block])))
    top, low = pl.ds(0, 128), pl.ds(128, PACK - 128)
    for i, q in enumerate(order_of_shares):
        swaps[i].wait_recv()
        block, small = rows(q, HALF), rows(q, PACK)
        for b in range(2):
            g_c[b, small, :] = packed(g_x[b, block, :])
        total = nt(g_c[0, small, :], sd_v[0]) + nt(g_c[1, small, :], sd_v[1])
        if i == 0:
            b_send[0] = total.astype(BF)
            from_left = go(to_ring(6, b_send.at[0, top], b_recv.at[0, top], right))
            from_right = go(to_ring(7, b_send.at[0, low], b_recv.at[0, low], left))
        elif i == 1:
            b_send[1, low, :] = total[128:].astype(BF)
            b_keep[top, :] = total[:128]
            left_low = go(to_ring(8, b_send.at[1, low], b_recv.at[1, low], right))
        elif i == 2:
            b_send[2, top, :] = total[:128].astype(BF)
            b_keep[low, :] = total[128:]
            right_top = go(to_ring(9, b_send.at[2, top], b_recv.at[2, top], left))
        else:
            b_own[...] = total

    def down_grad(b):
        for part in range(3):
            tall = slice(part * 256, (part + 1) * 256)
            td_v[0, tall, b * NAR : (b + 1) * NAR] = tn(s_hid[:, tall], g_c[b]).astype(BF)

    down_grad(0)
    from_left.wait_recv()
    b_send[1, top, :] = (b_keep[top, :] + b_recv[0, top, :].astype(F32)).astype(BF)
    left_top = go(to_ring(10, b_send.at[1, top], b_recv.at[1, top], right))
    from_right.wait_recv()
    b_send[2, low, :] = (b_keep[low, :] + b_recv[0, low, :].astype(F32)).astype(BF)
    right_low = go(to_ring(11, b_send.at[2, low], b_recv.at[2, low], left))
    down_grad(1)
    out_gd = pltpu.make_async_copy(td_v.at[0], gd_o, out_sem.at[1])
    out_gd.start()

    for one in (left_low, right_top, left_top, right_low):
        one.wait_recv()
    back = b_own[...] + b_recv[1].astype(F32) + b_recv[2].astype(F32)
    s_gate, s_up = s_pown[0], s_pown[1]
    sig = jax.nn.sigmoid(s_gate)

    def part_of(q, lower):
        return pl.ds(pl.multiple_of(q * PACK + lower * 128, SLOT), PACK - 128 if lower else 128)

    def share_rows(n, buf):
        def send(i, q, lower, p):
            block = buf.at[part_of(q, lower)]
            return go(to_ring(n + i, block, block, p))

        return send, [send(0, x, 0, right), send(1, x, 1, left)], [
            send(2, x, 1, right),
            send(3, x, 0, left),
        ]

    def pass_rows(send, first):
        first[0].wait_recv()
        one = send(4, left, 0, right)
        first[1].wait_recv()
        return [one, send(5, right, 1, left)]

    gr_v[own_share, :] = (back * s_up * sig * (1.0 + s_gate * (1.0 - sig))).astype(BF)
    g_sender, g_first, g_rest = share_rows(14, gr_v)
    ur_v[own_share, :] = (back * s_gate * sig).astype(BF)
    g_rest = g_rest + pass_rows(g_sender, g_first)
    u_sender, u_first, u_rest = share_rows(20, ur_v)
    for one in g_rest:
        one.wait_recv()

    u_rest = u_rest + pass_rows(u_sender, u_first)
    for b in range(2):
        for part in range(3):
            tall = slice(part * 256, (part + 1) * 256)
            td_v[1, tall, b * NAR : (b + 1) * NAR] = tn(gr_v[:, tall], s_c[b]).astype(BF)
    out_gg = pltpu.make_async_copy(td_v.at[1], gg_o, out_sem.at[2])
    out_gg.start()
    for one in u_rest:
        one.wait_recv()
    out_ur = pltpu.make_async_copy(ur_v, ur_o, out_sem.at[4])
    out_ur.start()

    all_sent(0, s_x.at[0, pl.ds(0, SR - 2 * SLOT)])
    all_sent(1, t_back.at[pl.ds(0, TR - SLOT)])
    all_sent(2, t_back.at[pl.ds(0, TR - SLOT)])
    all_sent(3, s_x.at[0, pl.ds(0, SR - 2 * SLOT)])
    all_sent(4, s_x.at[0, pl.ds(0, SR - 2 * SLOT)])
    for one in pending:
        one.wait_send()
    for one in (out_res, out_gd, out_gg, out_ur, out_sc):
        one.wait()


def finish(res, gg, gd, ur, sc, res_o, gg_o, gu_o, gd_o, ur_v, sc_v, gu_v, gg_v, gd_v, res_v, sem):
    def copy(n, src, dst):
        one = pltpu.make_async_copy(src, dst, sem.at[n])
        one.start()
        return one

    loads = [copy(0, ur, ur_v), copy(1, sc.at[0], sc_v.at[0]), copy(2, sc.at[1], sc_v.at[1])]
    through = [copy(3, gg, gg_v), copy(4, gd, gd_v), copy(5, res, res_v)]
    rest = []
    loads[0].wait()
    for b in range(2):
        loads[1 + b].wait()
        for part in range(3):
            tall = slice(part * 256, (part + 1) * 256)
            gu_v[b, tall, :] = tn(ur_v[:, tall], sc_v[b]).astype(BF)
        rest.append(copy(6 + b, gu_v.at[b], gu_o.at[0, :, pl.ds(b * NAR, NAR)]))
        if b == 0:
            for n, (held, out) in enumerate(((gg_v, gg_o.at[0]), (gd_v, gd_o.at[0]), (res_v, res_o))):
                through[n].wait()
                rest.append(copy(8 + n, held, out))
    for one in rest:
        one.wait()


def shards(tokens, ids, gates, order, tg, tu, td, sg, su, sd):
    vmem = pl.BlockSpec(memory_space=pltpu.VMEM)
    hbm = pl.BlockSpec(memory_space=pl.ANY)
    dma = pltpu.SemaphoreType.DMA

    def buf(*shape, dtype=BF):
        return pltpu.VMEM(shape, dtype)

    parts = pl.pallas_call(
        body,
        out_shape=(
            jax.ShapeDtypeStruct((TOK, COL), F32),
            jax.ShapeDtypeStruct((HID, COL), BF),
            jax.ShapeDtypeStruct((HID, COL), BF),
            jax.ShapeDtypeStruct((4 * PACK, HID), BF),
            jax.ShapeDtypeStruct((2, 4 * PACK, NAR), BF),
        ),
        in_specs=[vmem] * 3 + [hbm] * 7,
        out_specs=(hbm,) * 5,
        scratch_shapes=[
            buf(TOK, COL),
            buf(HID, 2 * COL),
            buf(HID, 2 * COL),
            buf(2, HID, COL),
            buf(HID, COL),
            buf(HID, COL),
            buf(2, HID, NAR),
            buf(TR, TOK),
            buf(TR, TOK),
            buf(4, TR, TOK),
            buf(4, TOK, TR),
            buf(2, TR, NAR),
            buf(TR, COL),
            buf(2, SR, NAR),
            buf(2, 4 * PACK, NAR),
            buf(2, TR, COL),
            buf(PACK, HALF),
            buf(HALF, PACK),
            buf(3, 2, PACK, HID),
            buf(2, PACK, HID, dtype=F32),
            buf(2, PACK, HID, dtype=F32),
            buf(3, 2, PACK, HID),
            buf(2, PACK, HID),
            buf(2, PACK, HID, dtype=F32),
            buf(2, PACK, HID),
            buf(4 * PACK, HID),
            buf(2 * PACK, HID),
            buf(2 * PACK, COL),
            buf(2 * PACK, COL),
            buf(TR, COL),
            buf(TR, COL),
            buf(4 * PACK, NAR),
            buf(4 * PACK, NAR),
            buf(SR, NAR),
            buf(2, TR, NAR),
            buf(TOK, COL, dtype=F32),
            buf(2, TR, NAR),
            buf(2, SR, NAR),
            buf(2, 4 * PACK, NAR),
            buf(3, PACK, HID),
            buf(PACK, HID, dtype=F32),
            buf(PACK, HID, dtype=F32),
            buf(3, PACK, HID),
            buf(4 * PACK, HID),
            buf(4 * PACK, HID),
            dma((9,)),
            dma((5,)),
            dma((5,)),
            dma((5,)),
            dma((16,)),
            dma((16,)),
            dma((26,)),
            dma((26,)),
        ],
        compiler_params=pltpu.CompilerParams(
            collective_id=0, has_side_effects=True, vmem_limit_bytes=60 << 20
        ),
        cost_estimate=pl.CostEstimate(
            flops=16_000_000_000, bytes_accessed=24_000_000, transcendentals=1_000_000
        ),
        name="distill",
    )(ids.T, gates.T, order.reshape(1, OWNERS), tokens, tg, tu, td, sg, su, sd)
    weight = jax.ShapeDtypeStruct((1, HID, COL), BF)
    return pl.pallas_call(
        finish,
        out_shape=(jax.ShapeDtypeStruct((TOK, COL), F32), weight, weight, weight),
        in_specs=[hbm] * 5,
        out_specs=(hbm,) * 4,
        scratch_shapes=[
            buf(4 * PACK, HID),
            buf(2, 4 * PACK, NAR),
            buf(2, HID, NAR),
            buf(HID, COL),
            buf(HID, COL),
            buf(TOK, COL, dtype=F32),
            dma((11,)),
        ],
        compiler_params=pltpu.CompilerParams(vmem_limit_bytes=60 << 20),
        cost_estimate=pl.CostEstimate(
            flops=1_600_000_000, bytes_accessed=13_000_000, transcendentals=0
        ),
        name="finish",
    )(*parts)


def solution(mesh):
    weights = P("expert", "replica", "group")
    return jax.shard_map(
        shards,
        mesh=mesh,
        in_specs=(P("expert", "group"), P("expert", None), P("expert", None), P()) + (weights,) * 6,
        out_specs=(P("expert", ("group", "replica")), weights, weights, weights),
        check_vma=False,
    )
```

```python
import jax
import jax.numpy as jnp
from jax import lax
from jax.experimental import pallas as pl
from jax.experimental.pallas import tpu as pltpu
from jax.sharding import PartitionSpec as P

MESH = pl.DeviceIdType.MESH
BF = jnp.bfloat16
F32 = jnp.float32
OWNERS = 32
TOK = 192
SLOT = 16
TR = OWNERS * SLOT
SR = 2 * TR
HALF = SR // 4
PACK = HALF // SLOT * (SLOT - 1)
HID = 768
COL = 1024
NAR = 512


def nn(a, b):
    return lax.dot_general(a, b, (((1,), (0,)), ((), ())), preferred_element_type=F32)


def nt(a, b):
    return lax.dot_general(a, b, (((1,), (1,)), ((), ())), preferred_element_type=F32)


def tn(a, b):
    return lax.dot_general(a, b, (((0,), (0,)), ((), ())), preferred_element_type=F32)


def hi_lo(v):
    hi = v.astype(BF)
    return hi, (v - hi.astype(F32)).astype(BF)


def body(
    ids,
    gates,
    order,
    tokens,
    tg,
    tu,
    td,
    sg,
    su,
    sd,
    res_o,
    gg_o,
    gd_o,
    ur_o,
    sc_o,
    tok_v,
    tg_v,
    tu_v,
    td_v,
    sg_v,
    su_v,
    sd_v,
    t_onehot,
    s_onehot,
    comb,
    comb_t,
    s_send,
    t_send,
    s_x,
    s_c,
    t_x,
    pack,
    unpack,
    s_psend,
    s_pown,
    s_pkeep,
    s_precv,
    t_psend,
    t_pown,
    t_precv,
    s_hid,
    t_hid,
    t_csend,
    t_crecv,
    t_ret,
    t_back,
    s_csend,
    s_crecv,
    s_ret,
    s_back,
    res_v,
    g_send,
    g_x,
    g_c,
    b_send,
    b_own,
    b_keep,
    b_recv,
    gr_v,
    ur_v,
    load_sem,
    out_sem,
    a2a_s,
    a2a_r,
    core_s,
    core_r,
    ring_s,
    ring_r,
):
    me = lax.axis_index("expert")
    r = lax.axis_index("replica")
    g = lax.axis_index("group")
    h = lax.rem(me, 2)
    x = h * 2 + g
    pair = me - h
    nr = 1 - r

    def place(e):
        z, y, hh = e // 8, lax.rem(e // 2, 4), lax.rem(e, 2)
        return 8 * lax.rem(z + y, 4) + 2 * z + hh

    def peer(e):
        return {"expert": e, "replica": r, "group": g}

    def ring(p):
        return {"expert": pair + p // 2, "replica": r, "group": lax.rem(p, 2)}

    right, left, opposite = lax.rem(x + 1, 4), lax.rem(x + 3, 4), lax.rem(x + 2, 4)
    near, across = h * 2 + 1 - g, 3 - x
    other_core = {"expert": me, "replica": nr, "group": g}
    partner = {"expert": me, "replica": r, "group": 1 - g}
    mine = place(me)

    def load(n, src, dst):
        return pltpu.make_async_copy(src, dst, load_sem.at[n])

    loads = [
        load(0, tokens.at[:, pl.ds(pl.multiple_of(r * COL, COL), COL)], tok_v),
        load(1, sg.at[0], sg_v),
        load(2, su.at[0], su_v),
        load(3, tg.at[0], tg_v),
        load(4, tu.at[0], tu_v),
        load(5, sd.at[0, :, pl.ds(0, NAR)], sd_v.at[0]),
        load(6, sd.at[0, :, pl.ds(NAR, NAR)], sd_v.at[1]),
        load(7, td.at[0, :, pl.ds(0, COL)], td_v.at[0]),
        load(8, td.at[0, :, pl.ds(COL, COL)], td_v.at[1]),
    ]
    for one in loads:
        one.start()

    barrier = pltpu.get_barrier_semaphore()

    @pl.loop(1, OWNERS)
    def _(k):
        pl.semaphore_signal(
            barrier, inc=1, device_id=peer(lax.rem(me + k, OWNERS)), device_id_type=MESH
        )

    pl.semaphore_signal(barrier, inc=1, device_id=other_core, device_id_type=MESH)
    pl.semaphore_signal(barrier, inc=1, device_id=partner, device_id_type=MESH)
    pl.semaphore_signal(barrier, inc=1, device_id=ring(across), device_id_type=MESH)
    expert_row = lax.broadcasted_iota(jnp.int32, (OWNERS, TOK), 0)
    member = jnp.zeros((OWNERS, TOK), F32)
    gate = jnp.zeros((OWNERS, TOK), F32)
    for k in range(8):
        same = ids[k : k + 1, :] == expert_row
        member = jnp.where(same, 1.0, member)
        gate = jnp.where(same, gates[k : k + 1, :], gate)
    upto = (
        lax.broadcasted_iota(jnp.int32, (TOK, TOK), 0)
        <= lax.broadcasted_iota(jnp.int32, (TOK, TOK), 1)
    ).astype(F32).astype(BF)
    rank = (member * nn(member.astype(BF), upto)).astype(BF)
    spread = (
        lax.shift_right_logical(lax.broadcasted_iota(jnp.int32, (TR, OWNERS), 0), 4)
        == lax.broadcasted_iota(jnp.int32, (TR, OWNERS), 1)
    ).astype(F32).astype(BF)
    turn = (
        lax.broadcasted_iota(jnp.int32, (OWNERS, OWNERS), 0) == order[0:1, :]
    ).astype(F32).astype(BF)
    s_spread = nt(spread, turn).astype(BF)
    want = ((lax.broadcasted_iota(jnp.int32, (TR, 1), 0) & (SLOT - 1)) + 1).astype(F32)
    s_hit = nn(s_spread, rank) == want
    s_onehot[...] = jnp.where(s_hit, 1.0, 0.0).astype(BF)
    loads[0].wait()
    for hh in range(2):
        s_send[hh] = nn(s_onehot[...], tok_v[:, hh * NAR : (hh + 1) * NAR]).astype(BF)
    pl.semaphore_wait(barrier, OWNERS + 2)

    def scatter(n, src_of, dst):
        @pl.loop(1, OWNERS)
        def _(k):
            e = lax.rem(me + k, OWNERS)
            pltpu.make_async_remote_copy(
                src_ref=src_of(e),
                dst_ref=dst,
                send_sem=a2a_s.at[n],
                recv_sem=a2a_r.at[n],
                device_id=peer(e),
                device_id_type=MESH,
            ).start()

    def scatter_share(n, q, src_of, dst):
        @pl.loop(0, 8)
        def _(k):
            turned = lax.rem(k + me, 8)
            z = turned // 2
            e = 8 * z + 2 * lax.rem(q + 4 - z, 4) + lax.rem(turned, 2)

            @pl.when(e != me)
            def _():
                pltpu.make_async_remote_copy(
                    src_ref=src_of(e),
                    dst_ref=dst,
                    send_sem=a2a_s.at[n],
                    recv_sem=a2a_r.at[n],
                    device_id=peer(e),
                    device_id_type=MESH,
                ).start()

    def all_sent(n, like):
        pltpu.make_async_copy(like, like, a2a_s.at[n]).wait()

    def all_here(n, like):
        pltpu.make_async_copy(like, like, a2a_r.at[n]).wait()

    def rows(e, size):
        return pl.ds(pl.multiple_of(e * size, size), size)

    s_rows, t_rows = rows(mine, 2 * SLOT), rows(mine, SLOT)
    m_rows = rows(me // 2, 2 * SLOT)
    scatter(0, lambda e: s_send.at[lax.rem(e, 2), rows(e // 2, 2 * SLOT)], s_x.at[r, s_rows])
    s_x[r, s_rows, :] = s_send[h, m_rows, :]
    t_hit = nn(spread, rank) == want
    t_onehot[...] = jnp.where(t_hit, 1.0, 0.0).astype(BF)
    t_send[...] = nn(t_onehot[...], tok_v[...]).astype(BF)
    scatter(1, lambda e: t_send.at[rows(e, SLOT)], t_x.at[r, t_rows])
    t_x[r, t_rows, :] = t_send[rows(me, SLOT), :]
    gate_hi, gate_lo = hi_lo(gate)
    s_hit = s_onehot[...].astype(F32)
    t_hit = t_onehot[...].astype(F32)
    comb[0] = (s_hit * nn(s_spread, gate_hi)).astype(BF)
    comb[1] = (s_hit * nn(s_spread, gate_lo)).astype(BF)
    comb[2] = (t_hit * -nn(spread, gate_hi)).astype(BF)
    comb[3] = (t_hit * -nn(spread, gate_lo)).astype(BF)
    same_token = (
        lax.broadcasted_iota(jnp.int32, (TOK, TOK), 0)
        == lax.broadcasted_iota(jnp.int32, (TOK, TOK), 1)
    ).astype(F32).astype(BF)
    for n in range(4):
        comb_t[n] = nt(same_token, comb[n]).astype(BF)

    def packed_place(shape, dim):
        slot = lax.broadcasted_iota(jnp.int32, shape, dim)
        inner = slot & (SLOT - 1)
        to = lax.shift_right_logical(slot, 4) * (SLOT - 1) + inner
        hit = (to == lax.broadcasted_iota(jnp.int32, shape, 1 - dim)) & (inner < SLOT - 1)
        return jnp.where(hit, 1.0, 0.0).astype(BF)

    pack[...] = packed_place((PACK, HALF), 1)
    unpack[...] = packed_place((HALF, PACK), 0)

    def packed(block):
        return nn(pack[...], block).astype(BF)

    def unpacked(block):
        return nn(unpack[...], block).astype(BF)

    def to_core(n, src, dst):
        return pltpu.make_async_remote_copy(
            src_ref=src,
            dst_ref=dst,
            send_sem=core_s.at[n],
            recv_sem=core_r.at[n],
            device_id=other_core,
            device_id_type=MESH,
        )

    def to_ring(n, src, dst, p):
        return pltpu.make_async_remote_copy(
            src_ref=src,
            dst_ref=dst,
            send_sem=ring_s.at[n],
            recv_sem=ring_r.at[n],
            device_id=ring(p),
            device_id_type=MESH,
        )

    pending = []

    def go(copy):
        copy.start()
        pending.append(copy)
        return copy

    all_here(0, s_x.at[0, pl.ds(0, SR - 2 * SLOT)])
    order_of_shares = (opposite, across, near, x)
    swaps = []
    for i, q in enumerate(order_of_shares):
        block = rows(q, HALF)
        swaps.append(go(to_core(i, s_x.at[r, block], s_x.at[r, block])))
    loads[1].wait()
    loads[2].wait()
    for i, q in enumerate(order_of_shares):
        swaps[i].wait_recv()
        block, small = rows(q, HALF), rows(q, PACK)
        for b in range(2):
            s_c[b, small, :] = packed(s_x[b, block, :])
        for n, w in enumerate((sg_v, su_v)):
            total = nt(s_c[0, small, :], w[:, :NAR]) + nt(s_c[1, small, :], w[:, NAR:])
            if i < 2:
                s_psend[i, n] = total.astype(BF)
            elif i == 2:
                s_pkeep[n] = total
            else:
                s_pown[n] = total
        if i == 0:
            first_sum = go(to_ring(0, s_psend.at[0], s_precv.at[0], across))

    out_sc = pltpu.make_async_copy(s_c, sc_o, out_sem.at[3])
    out_sc.start()

    all_here(1, t_x.at[0, pl.ds(0, TR - SLOT)])
    t_swaps = []
    for i, half in enumerate((1 - g, g)):
        block = rows(half, HALF)
        t_swaps.append(go(to_core(4 + i, t_x.at[r, block], t_x.at[r, block])))
    loads[3].wait()
    loads[4].wait()
    for i, half in enumerate((1 - g, g)):
        t_swaps[i].wait_recv()
        block = rows(half, HALF)
        t_rows_a, t_rows_b = packed(t_x[0, block, :]), packed(t_x[1, block, :])
        for n, w in enumerate((tg_v, tu_v)):
            total = nt(t_rows_a, w[:, :COL]) + nt(t_rows_b, w[:, COL:])
            if i == 0:
                t_psend[n] = total.astype(BF)
            else:
                t_pown[n] = total
        if i == 0:
            t_pre = go(
                pltpu.make_async_remote_copy(
                    src_ref=t_psend,
                    dst_ref=t_precv,
                    send_sem=ring_s.at[12],
                    recv_sem=ring_r.at[12],
                    device_id=partner,
                    device_id_type=MESH,
                )
            )
    first_sum.wait_recv()
    across_sum = go(to_ring(1, s_psend.at[1], s_precv.at[1], across))
    for n in range(2):
        s_psend[2, n] = (s_pkeep[n] + s_precv[0, n].astype(F32)).astype(BF)
    near_sum = go(to_ring(2, s_psend.at[2], s_precv.at[2], near))
    t_pre.wait_recv()
    t_gate = t_pown[0] + t_precv[0].astype(F32)
    t_up = t_pown[1] + t_precv[1].astype(F32)
    own_half = rows(g, PACK)
    other_half = rows(1 - g, PACK)
    t_hid[own_half, :] = (t_gate * jax.nn.sigmoid(t_gate) * t_up).astype(BF)
    t_share = go(
        pltpu.make_async_remote_copy(
            src_ref=t_hid.at[own_half],
            dst_ref=t_hid.at[own_half],
            send_sem=ring_s.at[13],
            recv_sem=ring_r.at[13],
            device_id=partner,
            device_id_type=MESH,
        )
    )

    loads[7].wait()
    loads[8].wait()
    t_csend[own_half, :] = nn(t_hid[own_half, :], td_v[nr]).astype(BF)
    t_outs = [go(to_core(6, t_csend.at[own_half], t_crecv.at[own_half]))]

    def teacher_back(half, one):
        one.wait_recv()
        block = rows(half, PACK)
        total = nn(t_hid[block, :], td_v[r]) + t_crecv[block, :].astype(F32)
        t_ret[rows(half, HALF), :] = unpacked(total.astype(BF))
        for q in (2 * half, 2 * half + 1):
            scatter_share(2, q, lambda e: t_ret.at[rows(place(e), SLOT)], t_back.at[rows(me, SLOT)])

    def part_of(q, lower):
        return pl.ds(pl.multiple_of(q * PACK + lower * 128, SLOT), PACK - 128 if lower else 128)

    def share_rows(n, buf):
        def send(i, q, lower, p):
            block = buf.at[part_of(q, lower)]
            return go(to_ring(n + i, block, block, p))

        return send, [send(0, x, 0, right), send(1, x, 1, left)], [
            send(2, x, 1, right),
            send(3, x, 0, left),
        ]

    def pass_rows(send, first):
        first[0].wait_recv()
        one = send(4, left, 0, right)
        first[1].wait_recv()
        return [one, send(5, right, 1, left)]

    across_sum.wait_recv()
    near_sum.wait_recv()
    for n in range(2):
        s_pown[n] = s_pown[n] + s_precv[1, n].astype(F32) + s_precv[2, n].astype(F32)
    s_gate, s_up = s_pown[0], s_pown[1]
    own_share = rows(x, PACK)
    s_hid[own_share, :] = (s_gate * jax.nn.sigmoid(s_gate) * s_up).astype(BF)
    h_sender, h_first, h_rest = share_rows(26, s_hid)

    loads[5].wait()
    loads[6].wait()
    s_outs = []

    def merged_part(i, q):
        block = rows(q, PACK)
        s_csend[block, :] = nn(s_hid[block, :], sd_v[nr]).astype(BF)
        s_outs.append(go(to_core(8 + i, s_csend.at[block], s_crecv.at[block])))

    def merged_back(i, q):
        s_outs[i].wait_recv()
        block = rows(q, PACK)
        total = nn(s_hid[block, :], sd_v[r]) + s_crecv[block, :].astype(F32)
        s_ret[rows(q, HALF), :] = unpacked(total.astype(BF))
        scatter_share(
            3, q, lambda e: s_ret.at[rows(place(e), 2 * SLOT)], s_back.at[h, m_rows]
        )

    t_share.wait_recv()
    t_csend[other_half, :] = nn(t_hid[other_half, :], td_v[nr]).astype(BF)
    t_outs.append(go(to_core(7, t_csend.at[other_half], t_crecv.at[other_half])))
    merged_part(0, x)
    h_far = pass_rows(h_sender, h_first)
    teacher_back(g, t_outs[0])
    teacher_back(1 - g, t_outs[1])
    t_back[rows(me, SLOT), :] = t_ret[t_rows, :]
    for one in h_rest:
        one.wait_recv()
    merged_part(1, near)
    merged_part(2, across)
    for one in h_far:
        one.wait_recv()
    merged_part(3, opposite)
    merged_back(0, x)
    merged_back(1, near)
    merged_back(2, across)
    merged_back(3, opposite)
    s_back[h, m_rows, :] = s_ret[s_rows, :]

    all_here(2, t_back.at[pl.ds(0, TR - SLOT)])
    all_here(3, s_x.at[0, pl.ds(0, SR - 2 * SLOT)])
    for hh in range(2):
        wide = slice(hh * NAR, (hh + 1) * NAR)
        back_s, back_t = s_back[hh], t_back[:, wide]
        residual = (
            nn(comb_t[0], back_s)
            + nn(comb_t[1], back_s)
            + nn(comb_t[2], back_t)
            + nn(comb_t[3], back_t)
        )
        res_v[:, wide] = residual
        res_hi, res_lo = hi_lo(residual)
        g_send[hh] = (
            nn(comb[0], res_hi) + nn(comb[0], res_lo) + nn(comb[1], res_hi)
        ).astype(BF)
    scatter(4, lambda e: g_send.at[lax.rem(e, 2), rows(e // 2, 2 * SLOT)], g_x.at[r, s_rows])
    g_x[r, s_rows, :] = g_send[h, m_rows, :]
    out_res = pltpu.make_async_copy(res_v, res_o, out_sem.at[0])
    out_res.start()

    all_here(4, g_x.at[0, pl.ds(0, SR - 2 * SLOT)])
    order_of_shares = (opposite, right, left, x)
    swaps = []
    for i, q in enumerate(order_of_shares):
        block = rows(q, HALF)
        swaps.append(go(to_core(12 + i, g_x.at[r, block], g_x.at[r, block])))
    top, low = pl.ds(0, 128), pl.ds(128, PACK - 128)
    for i, q in enumerate(order_of_shares):
        swaps[i].wait_recv()
        block, small = rows(q, HALF), rows(q, PACK)
        for b in range(2):
            g_c[b, small, :] = packed(g_x[b, block, :])
        total = nt(g_c[0, small, :], sd_v[0]) + nt(g_c[1, small, :], sd_v[1])
        if i == 0:
            b_send[0] = total.astype(BF)
            from_left = go(to_ring(6, b_send.at[0, top], b_recv.at[0, top], right))
            from_right = go(to_ring(7, b_send.at[0, low], b_recv.at[0, low], left))
        elif i == 1:
            b_send[1, low, :] = total[128:].astype(BF)
            b_keep[top, :] = total[:128]
            left_low = go(to_ring(8, b_send.at[1, low], b_recv.at[1, low], right))
        elif i == 2:
            b_send[2, top, :] = total[:128].astype(BF)
            b_keep[low, :] = total[128:]
            right_top = go(to_ring(9, b_send.at[2, top], b_recv.at[2, top], left))
        else:
            b_own[...] = total

    def down_grad(b):
        for part in range(3):
            tall = slice(part * 256, (part + 1) * 256)
            td_v[0, tall, b * NAR : (b + 1) * NAR] = tn(s_hid[:, tall], g_c[b]).astype(BF)

    down_grad(0)
    from_left.wait_recv()
    b_send[1, top, :] = (b_keep[top, :] + b_recv[0, top, :].astype(F32)).astype(BF)
    left_top = go(to_ring(10, b_send.at[1, top], b_recv.at[1, top], right))
    from_right.wait_recv()
    b_send[2, low, :] = (b_keep[low, :] + b_recv[0, low, :].astype(F32)).astype(BF)
    right_low = go(to_ring(11, b_send.at[2, low], b_recv.at[2, low], left))
    down_grad(1)
    out_gd = pltpu.make_async_copy(td_v.at[0], gd_o, out_sem.at[1])
    out_gd.start()

    for one in (left_low, right_top, left_top, right_low):
        one.wait_recv()
    back = b_own[...] + b_recv[1].astype(F32) + b_recv[2].astype(F32)
    s_gate, s_up = s_pown[0], s_pown[1]
    sig = jax.nn.sigmoid(s_gate)

    gr_v[own_share, :] = (back * s_up * sig * (1.0 + s_gate * (1.0 - sig))).astype(BF)
    g_sender, g_first, g_rest = share_rows(14, gr_v)
    ur_v[own_share, :] = (back * s_gate * sig).astype(BF)
    g_rest = g_rest + pass_rows(g_sender, g_first)
    u_sender, u_first, u_rest = share_rows(20, ur_v)
    for one in g_rest:
        one.wait_recv()

    u_rest = u_rest + pass_rows(u_sender, u_first)
    for b in range(2):
        for part in range(3):
            tall = slice(part * 256, (part + 1) * 256)
            td_v[1, tall, b * NAR : (b + 1) * NAR] = tn(gr_v[:, tall], s_c[b]).astype(BF)
    out_gg = pltpu.make_async_copy(td_v.at[1], gg_o, out_sem.at[2])
    out_gg.start()
    for one in u_rest:
        one.wait_recv()
    out_ur = pltpu.make_async_copy(ur_v, ur_o, out_sem.at[4])
    out_ur.start()

    all_sent(0, s_x.at[0, pl.ds(0, SR - 2 * SLOT)])
    all_sent(1, t_back.at[pl.ds(0, TR - SLOT)])
    all_sent(2, t_back.at[pl.ds(0, TR - SLOT)])
    all_sent(3, s_x.at[0, pl.ds(0, SR - 2 * SLOT)])
    all_sent(4, s_x.at[0, pl.ds(0, SR - 2 * SLOT)])
    for one in pending:
        one.wait_send()
    for one in (out_res, out_gd, out_gg, out_ur, out_sc):
        one.wait()


def finish(res, gg, gd, ur, sc, res_o, gg_o, gu_o, gd_o, ur_v, sc_v, gu_v, gg_v, gd_v, res_v, sem):
    def copy(n, src, dst):
        one = pltpu.make_async_copy(src, dst, sem.at[n])
        one.start()
        return one

    loads = [copy(0, ur, ur_v), copy(1, sc.at[0], sc_v.at[0]), copy(2, sc.at[1], sc_v.at[1])]
    through = [copy(3, gg, gg_v), copy(4, gd, gd_v), copy(5, res, res_v)]
    rest = []
    loads[0].wait()
    for b in range(2):
        loads[1 + b].wait()
        for part in range(3):
            tall = slice(part * 256, (part + 1) * 256)
            gu_v[b, tall, :] = tn(ur_v[:, tall], sc_v[b]).astype(BF)
        rest.append(copy(6 + b, gu_v.at[b], gu_o.at[0, :, pl.ds(b * NAR, NAR)]))
        if b == 0:
            for n, (held, out) in enumerate(((gg_v, gg_o.at[0]), (gd_v, gd_o.at[0]), (res_v, res_o))):
                through[n].wait()
                rest.append(copy(8 + n, held, out))
    for one in rest:
        one.wait()


def shards(tokens, ids, gates, order, tg, tu, td, sg, su, sd):
    vmem = pl.BlockSpec(memory_space=pltpu.VMEM)
    hbm = pl.BlockSpec(memory_space=pl.ANY)
    dma = pltpu.SemaphoreType.DMA

    def buf(*shape, dtype=BF):
        return pltpu.VMEM(shape, dtype)

    parts = pl.pallas_call(
        body,
        out_shape=(
            jax.ShapeDtypeStruct((TOK, COL), F32),
            jax.ShapeDtypeStruct((HID, COL), BF),
            jax.ShapeDtypeStruct((HID, COL), BF),
            jax.ShapeDtypeStruct((4 * PACK, HID), BF),
            jax.ShapeDtypeStruct((2, 4 * PACK, NAR), BF),
        ),
        in_specs=[vmem] * 3 + [hbm] * 7,
        out_specs=(hbm,) * 5,
        scratch_shapes=[
            buf(TOK, COL),
            buf(HID, 2 * COL),
            buf(HID, 2 * COL),
            buf(2, HID, COL),
            buf(HID, COL),
            buf(HID, COL),
            buf(2, HID, NAR),
            buf(TR, TOK),
            buf(TR, TOK),
            buf(4, TR, TOK),
            buf(4, TOK, TR),
            buf(2, TR, NAR),
            buf(TR, COL),
            buf(2, SR, NAR),
            buf(2, 4 * PACK, NAR),
            buf(2, TR, COL),
            buf(PACK, HALF),
            buf(HALF, PACK),
            buf(3, 2, PACK, HID),
            buf(2, PACK, HID, dtype=F32),
            buf(2, PACK, HID, dtype=F32),
            buf(3, 2, PACK, HID),
            buf(2, PACK, HID),
            buf(2, PACK, HID, dtype=F32),
            buf(2, PACK, HID),
            buf(4 * PACK, HID),
            buf(2 * PACK, HID),
            buf(2 * PACK, COL),
            buf(2 * PACK, COL),
            buf(TR, COL),
            buf(TR, COL),
            buf(4 * PACK, NAR),
            buf(4 * PACK, NAR),
            buf(SR, NAR),
            buf(2, TR, NAR),
            buf(TOK, COL, dtype=F32),
            buf(2, TR, NAR),
            buf(2, SR, NAR),
            buf(2, 4 * PACK, NAR),
            buf(3, PACK, HID),
            buf(PACK, HID, dtype=F32),
            buf(PACK, HID, dtype=F32),
            buf(3, PACK, HID),
            buf(4 * PACK, HID),
            buf(4 * PACK, HID),
            dma((9,)),
            dma((5,)),
            dma((5,)),
            dma((5,)),
            dma((16,)),
            dma((16,)),
            dma((32,)),
            dma((32,)),
        ],
        compiler_params=pltpu.CompilerParams(
            collective_id=0, has_side_effects=True, vmem_limit_bytes=60 << 20
        ),
        cost_estimate=pl.CostEstimate(
            flops=16_000_000_000, bytes_accessed=24_000_000, transcendentals=1_000_000
        ),
        name="distill",
    )(ids.T, gates.T, order.reshape(1, OWNERS), tokens, tg, tu, td, sg, su, sd)
    weight = jax.ShapeDtypeStruct((1, HID, COL), BF)
    return pl.pallas_call(
        finish,
        out_shape=(jax.ShapeDtypeStruct((TOK, COL), F32), weight, weight, weight),
        in_specs=[hbm] * 5,
        out_specs=(hbm,) * 4,
        scratch_shapes=[
            buf(4 * PACK, HID),
            buf(2, 4 * PACK, NAR),
            buf(2, HID, NAR),
            buf(HID, COL),
            buf(HID, COL),
            buf(TOK, COL, dtype=F32),
            dma((11,)),
        ],
        compiler_params=pltpu.CompilerParams(vmem_limit_bytes=60 << 20),
        cost_estimate=pl.CostEstimate(
            flops=1_600_000_000, bytes_accessed=13_000_000, transcendentals=0
        ),
        name="finish",
    )(*parts)


def solution(mesh):
    weights = P("expert", "replica", "group")
    return jax.shard_map(
        shards,
        mesh=mesh,
        in_specs=(P("expert", "group"), P("expert", None), P("expert", None), P()) + (weights,) * 6,
        out_specs=(P("expert", ("group", "replica")), weights, weights, weights),
        check_vma=False,
    )
```

```python
import jax
import jax.numpy as jnp
from jax import lax
from jax.experimental import pallas as pl
from jax.experimental.pallas import tpu as pltpu
from jax.sharding import PartitionSpec as P

MESH = pl.DeviceIdType.MESH
BF = jnp.bfloat16
F32 = jnp.float32
OWNERS = 32
TOK = 192
SLOT = 16
TR = OWNERS * SLOT
SR = 2 * TR
HALF = SR // 4
PACK = HALF // SLOT * (SLOT - 1)
HID = 768
COL = 1024
NAR = 512


def nn(a, b):
    return lax.dot_general(a, b, (((1,), (0,)), ((), ())), preferred_element_type=F32)


def nt(a, b):
    return lax.dot_general(a, b, (((1,), (1,)), ((), ())), preferred_element_type=F32)


def tn(a, b):
    return lax.dot_general(a, b, (((0,), (0,)), ((), ())), preferred_element_type=F32)


def hi_lo(v):
    hi = v.astype(BF)
    return hi, (v - hi.astype(F32)).astype(BF)


def body(
    ids,
    gates,
    order,
    tokens,
    tg,
    tu,
    td,
    sg,
    su,
    sd,
    res_o,
    gg_o,
    gd_o,
    ur_o,
    sc_o,
    tok_v,
    tg_v,
    tu_v,
    td_v,
    sg_v,
    su_v,
    sd_v,
    t_onehot,
    s_onehot,
    comb,
    comb_t,
    s_send,
    t_send,
    s_x,
    s_c,
    t_x,
    pack,
    unpack,
    s_psend,
    s_pown,
    s_pkeep,
    s_precv,
    t_psend,
    t_pown,
    t_precv,
    s_hid,
    t_hid,
    t_csend,
    t_crecv,
    t_ret,
    t_back,
    s_csend,
    s_crecv,
    s_ret,
    s_back,
    res_v,
    g_send,
    g_x,
    g_c,
    b_send,
    b_own,
    b_keep,
    b_recv,
    gr_v,
    ur_v,
    load_sem,
    out_sem,
    a2a_s,
    a2a_r,
    core_s,
    core_r,
    ring_s,
    ring_r,
):
    me = lax.axis_index("expert")
    r = lax.axis_index("replica")
    g = lax.axis_index("group")
    h = lax.rem(me, 2)
    x = h * 2 + g
    pair = me - h
    nr = 1 - r

    def place(e):
        z, y, hh = e // 8, lax.rem(e // 2, 4), lax.rem(e, 2)
        return 8 * lax.rem(z + y, 4) + 2 * z + hh

    def peer(e):
        return {"expert": e, "replica": r, "group": g}

    def ring(p):
        return {"expert": pair + p // 2, "replica": r, "group": lax.rem(p, 2)}

    right, left, opposite = lax.rem(x + 1, 4), lax.rem(x + 3, 4), lax.rem(x + 2, 4)
    near, across = h * 2 + 1 - g, 3 - x
    other_core = {"expert": me, "replica": nr, "group": g}
    partner = {"expert": me, "replica": r, "group": 1 - g}
    mine = place(me)

    def load(n, src, dst):
        return pltpu.make_async_copy(src, dst, load_sem.at[n])

    loads = [
        load(0, tokens.at[:, pl.ds(pl.multiple_of(r * COL, COL), COL)], tok_v),
        load(1, sg.at[0], sg_v),
        load(2, su.at[0], su_v),
        load(3, tg.at[0], tg_v),
        load(4, tu.at[0], tu_v),
        load(5, sd.at[0, :, pl.ds(0, NAR)], sd_v.at[0]),
        load(6, sd.at[0, :, pl.ds(NAR, NAR)], sd_v.at[1]),
        load(7, td.at[0, :, pl.ds(0, COL)], td_v.at[0]),
        load(8, td.at[0, :, pl.ds(COL, COL)], td_v.at[1]),
    ]
    for one in loads:
        one.start()

    barrier = pltpu.get_barrier_semaphore()

    @pl.loop(1, OWNERS)
    def _(k):
        pl.semaphore_signal(
            barrier, inc=1, device_id=peer(lax.rem(me + k, OWNERS)), device_id_type=MESH
        )

    pl.semaphore_signal(barrier, inc=1, device_id=other_core, device_id_type=MESH)
    pl.semaphore_signal(barrier, inc=1, device_id=partner, device_id_type=MESH)
    pl.semaphore_signal(barrier, inc=1, device_id=ring(across), device_id_type=MESH)
    expert_row = lax.broadcasted_iota(jnp.int32, (OWNERS, TOK), 0)
    member = jnp.zeros((OWNERS, TOK), F32)
    gate = jnp.zeros((OWNERS, TOK), F32)
    for k in range(8):
        same = ids[k : k + 1, :] == expert_row
        member = jnp.where(same, 1.0, member)
        gate = jnp.where(same, gates[k : k + 1, :], gate)
    upto = (
        lax.broadcasted_iota(jnp.int32, (TOK, TOK), 0)
        <= lax.broadcasted_iota(jnp.int32, (TOK, TOK), 1)
    ).astype(F32).astype(BF)
    rank = (member * nn(member.astype(BF), upto)).astype(BF)
    spread = (
        lax.shift_right_logical(lax.broadcasted_iota(jnp.int32, (TR, OWNERS), 0), 4)
        == lax.broadcasted_iota(jnp.int32, (TR, OWNERS), 1)
    ).astype(F32).astype(BF)
    turn = (
        lax.broadcasted_iota(jnp.int32, (OWNERS, OWNERS), 0) == order[0:1, :]
    ).astype(F32).astype(BF)
    s_spread = nt(spread, turn).astype(BF)
    want = ((lax.broadcasted_iota(jnp.int32, (TR, 1), 0) & (SLOT - 1)) + 1).astype(F32)
    s_hit = nn(s_spread, rank) == want
    s_onehot[...] = jnp.where(s_hit, 1.0, 0.0).astype(BF)
    loads[0].wait()
    for hh in range(2):
        s_send[hh] = nn(s_onehot[...], tok_v[:, hh * NAR : (hh + 1) * NAR]).astype(BF)
    pl.semaphore_wait(barrier, OWNERS + 2)

    def scatter(n, src_of, dst):
        @pl.loop(1, OWNERS)
        def _(k):
            e = lax.rem(me + k, OWNERS)
            pltpu.make_async_remote_copy(
                src_ref=src_of(e),
                dst_ref=dst,
                send_sem=a2a_s.at[n],
                recv_sem=a2a_r.at[n],
                device_id=peer(e),
                device_id_type=MESH,
            ).start()

    def scatter_share(n, q, src_of, dst):
        @pl.loop(0, 8)
        def _(k):
            turned = lax.rem(k + me, 8)
            z = turned // 2
            e = 8 * z + 2 * lax.rem(q + 4 - z, 4) + lax.rem(turned, 2)

            @pl.when(e != me)
            def _():
                pltpu.make_async_remote_copy(
                    src_ref=src_of(e),
                    dst_ref=dst,
                    send_sem=a2a_s.at[n],
                    recv_sem=a2a_r.at[n],
                    device_id=peer(e),
                    device_id_type=MESH,
                ).start()

    def all_sent(n, like):
        pltpu.make_async_copy(like, like, a2a_s.at[n]).wait()

    def all_here(n, like):
        pltpu.make_async_copy(like, like, a2a_r.at[n]).wait()

    def rows(e, size):
        return pl.ds(pl.multiple_of(e * size, size), size)

    s_rows, t_rows = rows(mine, 2 * SLOT), rows(mine, SLOT)
    m_rows = rows(me // 2, 2 * SLOT)
    scatter(0, lambda e: s_send.at[lax.rem(e, 2), rows(e // 2, 2 * SLOT)], s_x.at[r, s_rows])
    s_x[r, s_rows, :] = s_send[h, m_rows, :]
    t_hit = nn(spread, rank) == want
    t_onehot[...] = jnp.where(t_hit, 1.0, 0.0).astype(BF)
    t_send[...] = nn(t_onehot[...], tok_v[...]).astype(BF)
    scatter(1, lambda e: t_send.at[rows(e, SLOT)], t_x.at[r, t_rows])
    t_x[r, t_rows, :] = t_send[rows(me, SLOT), :]
    gate_hi, gate_lo = hi_lo(gate)
    s_hit = s_onehot[...].astype(F32)
    t_hit = t_onehot[...].astype(F32)
    comb[0] = (s_hit * nn(s_spread, gate_hi)).astype(BF)
    comb[1] = (s_hit * nn(s_spread, gate_lo)).astype(BF)
    comb[2] = (t_hit * -nn(spread, gate_hi)).astype(BF)
    comb[3] = (t_hit * -nn(spread, gate_lo)).astype(BF)
    same_token = (
        lax.broadcasted_iota(jnp.int32, (TOK, TOK), 0)
        == lax.broadcasted_iota(jnp.int32, (TOK, TOK), 1)
    ).astype(F32).astype(BF)
    for n in range(4):
        comb_t[n] = nt(same_token, comb[n]).astype(BF)

    def packed_place(shape, dim):
        slot = lax.broadcasted_iota(jnp.int32, shape, dim)
        inner = slot & (SLOT - 1)
        to = lax.shift_right_logical(slot, 4) * (SLOT - 1) + inner
        hit = (to == lax.broadcasted_iota(jnp.int32, shape, 1 - dim)) & (inner < SLOT - 1)
        return jnp.where(hit, 1.0, 0.0).astype(BF)

    pack[...] = packed_place((PACK, HALF), 1)
    unpack[...] = packed_place((HALF, PACK), 0)

    def packed(block):
        return nn(pack[...], block).astype(BF)

    def unpacked(block):
        return nn(unpack[...], block).astype(BF)

    def to_core(n, src, dst):
        return pltpu.make_async_remote_copy(
            src_ref=src,
            dst_ref=dst,
            send_sem=core_s.at[n],
            recv_sem=core_r.at[n],
            device_id=other_core,
            device_id_type=MESH,
        )

    def to_ring(n, src, dst, p):
        return pltpu.make_async_remote_copy(
            src_ref=src,
            dst_ref=dst,
            send_sem=ring_s.at[n],
            recv_sem=ring_r.at[n],
            device_id=ring(p),
            device_id_type=MESH,
        )

    pending = []

    def go(copy):
        copy.start()
        pending.append(copy)
        return copy

    all_here(0, s_x.at[0, pl.ds(0, SR - 2 * SLOT)])
    order_of_shares = (opposite, across, near, x)
    swaps = []
    for i, q in enumerate(order_of_shares):
        block = rows(q, HALF)
        swaps.append(go(to_core(i, s_x.at[r, block], s_x.at[r, block])))
    loads[1].wait()
    loads[2].wait()
    for i, q in enumerate(order_of_shares):
        swaps[i].wait_recv()
        block, small = rows(q, HALF), rows(q, PACK)
        for b in range(2):
            s_c[b, small, :] = packed(s_x[b, block, :])
        for n, w in enumerate((sg_v, su_v)):
            total = nt(s_c[0, small, :], w[:, :NAR]) + nt(s_c[1, small, :], w[:, NAR:])
            if i < 2:
                s_psend[i, n] = total.astype(BF)
            elif i == 2:
                s_pkeep[n] = total
            else:
                s_pown[n] = total
        if i == 0:
            first_sum = go(to_ring(0, s_psend.at[0], s_precv.at[0], across))

    out_sc = pltpu.make_async_copy(s_c, sc_o, out_sem.at[3])
    out_sc.start()

    all_here(1, t_x.at[0, pl.ds(0, TR - SLOT)])
    t_swaps = []
    for i, half in enumerate((1 - g, g)):
        block = rows(half, HALF)
        t_swaps.append(go(to_core(4 + i, t_x.at[r, block], t_x.at[r, block])))
    loads[3].wait()
    loads[4].wait()
    for i, half in enumerate((1 - g, g)):
        t_swaps[i].wait_recv()
        block = rows(half, HALF)
        t_rows_a, t_rows_b = packed(t_x[0, block, :]), packed(t_x[1, block, :])
        for n, w in enumerate((tg_v, tu_v)):
            total = nt(t_rows_a, w[:, :COL]) + nt(t_rows_b, w[:, COL:])
            if i == 0:
                t_psend[n] = total.astype(BF)
            else:
                t_pown[n] = total
        if i == 0:
            t_pre = go(
                pltpu.make_async_remote_copy(
                    src_ref=t_psend,
                    dst_ref=t_precv,
                    send_sem=ring_s.at[12],
                    recv_sem=ring_r.at[12],
                    device_id=partner,
                    device_id_type=MESH,
                )
            )
    first_sum.wait_recv()
    across_sum = go(to_ring(1, s_psend.at[1], s_precv.at[1], across))
    for n in range(2):
        s_psend[2, n] = (s_pkeep[n] + s_precv[0, n].astype(F32)).astype(BF)
    near_sum = go(to_ring(2, s_psend.at[2], s_precv.at[2], near))
    t_pre.wait_recv()
    t_gate = t_pown[0] + t_precv[0].astype(F32)
    t_up = t_pown[1] + t_precv[1].astype(F32)
    own_half = rows(g, PACK)
    other_half = rows(1 - g, PACK)
    t_hid[own_half, :] = (t_gate * jax.nn.sigmoid(t_gate) * t_up).astype(BF)
    t_share = go(
        pltpu.make_async_remote_copy(
            src_ref=t_hid.at[own_half],
            dst_ref=t_hid.at[own_half],
            send_sem=ring_s.at[13],
            recv_sem=ring_r.at[13],
            device_id=partner,
            device_id_type=MESH,
        )
    )

    loads[7].wait()
    loads[8].wait()
    t_csend[own_half, :] = nn(t_hid[own_half, :], td_v[nr]).astype(BF)
    t_outs = [go(to_core(6, t_csend.at[own_half], t_crecv.at[own_half]))]

    def teacher_back(half, one):
        one.wait_recv()
        block = rows(half, PACK)
        total = nn(t_hid[block, :], td_v[r]) + t_crecv[block, :].astype(F32)
        t_ret[rows(half, HALF), :] = unpacked(total.astype(BF))
        for q in (2 * half, 2 * half + 1):
            scatter_share(2, q, lambda e: t_ret.at[rows(place(e), SLOT)], t_back.at[rows(me, SLOT)])

    def part_of(q, lower):
        return pl.ds(pl.multiple_of(q * PACK + lower * 128, SLOT), PACK - 128 if lower else 128)

    def share_rows(n, buf):
        def send(i, q, lower, p):
            block = buf.at[part_of(q, lower)]
            return go(to_ring(n + i, block, block, p))

        return send, [send(0, x, 0, right), send(1, x, 1, left)], [
            send(2, x, 1, right),
            send(3, x, 0, left),
        ]

    def pass_rows(send, first):
        first[0].wait_recv()
        one = send(4, left, 0, right)
        first[1].wait_recv()
        return [one, send(5, right, 1, left)]

    across_sum.wait_recv()
    near_sum.wait_recv()
    for n in range(2):
        s_pown[n] = s_pown[n] + s_precv[1, n].astype(F32) + s_precv[2, n].astype(F32)
    s_gate, s_up = s_pown[0], s_pown[1]
    own_share = rows(x, PACK)
    s_hid[own_share, :] = (s_gate * jax.nn.sigmoid(s_gate) * s_up).astype(BF)
    h_sender, h_first, h_rest = share_rows(26, s_hid)

    loads[5].wait()
    loads[6].wait()
    s_outs = []

    def merged_part(i, q):
        block = rows(q, PACK)
        s_csend[block, :] = nn(s_hid[block, :], sd_v[nr]).astype(BF)
        s_outs.append(go(to_core(8 + i, s_csend.at[block], s_crecv.at[block])))

    def merged_back(i, q):
        s_outs[i].wait_recv()
        block = rows(q, PACK)
        total = nn(s_hid[block, :], sd_v[r]) + s_crecv[block, :].astype(F32)
        s_ret[rows(q, HALF), :] = unpacked(total.astype(BF))
        scatter_share(
            3, q, lambda e: s_ret.at[rows(place(e), 2 * SLOT)], s_back.at[h, m_rows]
        )

    t_share.wait_recv()
    t_csend[other_half, :] = nn(t_hid[other_half, :], td_v[nr]).astype(BF)
    t_outs.append(go(to_core(7, t_csend.at[other_half], t_crecv.at[other_half])))
    merged_part(0, x)
    h_far = pass_rows(h_sender, h_first)
    for one in h_rest:
        one.wait_recv()
    merged_part(1, near)
    merged_part(2, across)
    for one in h_far:
        one.wait_recv()
    merged_part(3, opposite)
    teacher_back(g, t_outs[0])
    teacher_back(1 - g, t_outs[1])
    t_back[rows(me, SLOT), :] = t_ret[t_rows, :]
    merged_back(0, x)
    merged_back(1, near)
    merged_back(2, across)
    merged_back(3, opposite)
    s_back[h, m_rows, :] = s_ret[s_rows, :]

    all_here(2, t_back.at[pl.ds(0, TR - SLOT)])
    all_here(3, s_x.at[0, pl.ds(0, SR - 2 * SLOT)])
    for hh in range(2):
        wide = slice(hh * NAR, (hh + 1) * NAR)
        back_s, back_t = s_back[hh], t_back[:, wide]
        residual = (
            nn(comb_t[0], back_s)
            + nn(comb_t[1], back_s)
            + nn(comb_t[2], back_t)
            + nn(comb_t[3], back_t)
        )
        res_v[:, wide] = residual
        res_hi, res_lo = hi_lo(residual)
        g_send[hh] = (
            nn(comb[0], res_hi) + nn(comb[0], res_lo) + nn(comb[1], res_hi)
        ).astype(BF)
    scatter(4, lambda e: g_send.at[lax.rem(e, 2), rows(e // 2, 2 * SLOT)], g_x.at[r, s_rows])
    g_x[r, s_rows, :] = g_send[h, m_rows, :]
    out_res = pltpu.make_async_copy(res_v, res_o, out_sem.at[0])
    out_res.start()

    all_here(4, g_x.at[0, pl.ds(0, SR - 2 * SLOT)])
    order_of_shares = (opposite, right, left, x)
    swaps = []
    for i, q in enumerate(order_of_shares):
        block = rows(q, HALF)
        swaps.append(go(to_core(12 + i, g_x.at[r, block], g_x.at[r, block])))
    top, low = pl.ds(0, 128), pl.ds(128, PACK - 128)
    for i, q in enumerate(order_of_shares):
        swaps[i].wait_recv()
        block, small = rows(q, HALF), rows(q, PACK)
        for b in range(2):
            g_c[b, small, :] = packed(g_x[b, block, :])
        total = nt(g_c[0, small, :], sd_v[0]) + nt(g_c[1, small, :], sd_v[1])
        if i == 0:
            b_send[0] = total.astype(BF)
            from_left = go(to_ring(6, b_send.at[0, top], b_recv.at[0, top], right))
            from_right = go(to_ring(7, b_send.at[0, low], b_recv.at[0, low], left))
        elif i == 1:
            b_send[1, low, :] = total[128:].astype(BF)
            b_keep[top, :] = total[:128]
            left_low = go(to_ring(8, b_send.at[1, low], b_recv.at[1, low], right))
        elif i == 2:
            b_send[2, top, :] = total[:128].astype(BF)
            b_keep[low, :] = total[128:]
            right_top = go(to_ring(9, b_send.at[2, top], b_recv.at[2, top], left))
        else:
            b_own[...] = total

    def down_grad(b):
        for part in range(3):
            tall = slice(part * 256, (part + 1) * 256)
            td_v[0, tall, b * NAR : (b + 1) * NAR] = tn(s_hid[:, tall], g_c[b]).astype(BF)

    down_grad(0)
    from_left.wait_recv()
    b_send[1, top, :] = (b_keep[top, :] + b_recv[0, top, :].astype(F32)).astype(BF)
    left_top = go(to_ring(10, b_send.at[1, top], b_recv.at[1, top], right))
    from_right.wait_recv()
    b_send[2, low, :] = (b_keep[low, :] + b_recv[0, low, :].astype(F32)).astype(BF)
    right_low = go(to_ring(11, b_send.at[2, low], b_recv.at[2, low], left))
    down_grad(1)
    out_gd = pltpu.make_async_copy(td_v.at[0], gd_o, out_sem.at[1])
    out_gd.start()

    for one in (left_low, right_top, left_top, right_low):
        one.wait_recv()
    back = b_own[...] + b_recv[1].astype(F32) + b_recv[2].astype(F32)
    s_gate, s_up = s_pown[0], s_pown[1]
    sig = jax.nn.sigmoid(s_gate)

    gr_v[own_share, :] = (back * s_up * sig * (1.0 + s_gate * (1.0 - sig))).astype(BF)
    g_sender, g_first, g_rest = share_rows(14, gr_v)
    ur_v[own_share, :] = (back * s_gate * sig).astype(BF)
    g_rest = g_rest + pass_rows(g_sender, g_first)
    u_sender, u_first, u_rest = share_rows(20, ur_v)
    for one in g_rest:
        one.wait_recv()

    u_rest = u_rest + pass_rows(u_sender, u_first)
    for b in range(2):
        for part in range(3):
            tall = slice(part * 256, (part + 1) * 256)
            td_v[1, tall, b * NAR : (b + 1) * NAR] = tn(gr_v[:, tall], s_c[b]).astype(BF)
    out_gg = pltpu.make_async_copy(td_v.at[1], gg_o, out_sem.at[2])
    out_gg.start()
    for one in u_rest:
        one.wait_recv()
    out_ur = pltpu.make_async_copy(ur_v, ur_o, out_sem.at[4])
    out_ur.start()

    all_sent(0, s_x.at[0, pl.ds(0, SR - 2 * SLOT)])
    all_sent(1, t_back.at[pl.ds(0, TR - SLOT)])
    all_sent(2, t_back.at[pl.ds(0, TR - SLOT)])
    all_sent(3, s_x.at[0, pl.ds(0, SR - 2 * SLOT)])
    all_sent(4, s_x.at[0, pl.ds(0, SR - 2 * SLOT)])
    for one in pending:
        one.wait_send()
    for one in (out_res, out_gd, out_gg, out_ur, out_sc):
        one.wait()


def finish(res, gg, gd, ur, sc, res_o, gg_o, gu_o, gd_o, ur_v, sc_v, gu_v, gg_v, gd_v, res_v, sem):
    def copy(n, src, dst):
        one = pltpu.make_async_copy(src, dst, sem.at[n])
        one.start()
        return one

    loads = [copy(0, ur, ur_v), copy(1, sc.at[0], sc_v.at[0]), copy(2, sc.at[1], sc_v.at[1])]
    through = [copy(3, gg, gg_v), copy(4, gd, gd_v), copy(5, res, res_v)]
    rest = []
    loads[0].wait()
    for b in range(2):
        loads[1 + b].wait()
        for part in range(3):
            tall = slice(part * 256, (part + 1) * 256)
            gu_v[b, tall, :] = tn(ur_v[:, tall], sc_v[b]).astype(BF)
        rest.append(copy(6 + b, gu_v.at[b], gu_o.at[0, :, pl.ds(b * NAR, NAR)]))
        if b == 0:
            for n, (held, out) in enumerate(((gg_v, gg_o.at[0]), (gd_v, gd_o.at[0]), (res_v, res_o))):
                through[n].wait()
                rest.append(copy(8 + n, held, out))
    for one in rest:
        one.wait()


def shards(tokens, ids, gates, order, tg, tu, td, sg, su, sd):
    vmem = pl.BlockSpec(memory_space=pltpu.VMEM)
    hbm = pl.BlockSpec(memory_space=pl.ANY)
    dma = pltpu.SemaphoreType.DMA

    def buf(*shape, dtype=BF):
        return pltpu.VMEM(shape, dtype)

    parts = pl.pallas_call(
        body,
        out_shape=(
            jax.ShapeDtypeStruct((TOK, COL), F32),
            jax.ShapeDtypeStruct((HID, COL), BF),
            jax.ShapeDtypeStruct((HID, COL), BF),
            jax.ShapeDtypeStruct((4 * PACK, HID), BF),
            jax.ShapeDtypeStruct((2, 4 * PACK, NAR), BF),
        ),
        in_specs=[vmem] * 3 + [hbm] * 7,
        out_specs=(hbm,) * 5,
        scratch_shapes=[
            buf(TOK, COL),
            buf(HID, 2 * COL),
            buf(HID, 2 * COL),
            buf(2, HID, COL),
            buf(HID, COL),
            buf(HID, COL),
            buf(2, HID, NAR),
            buf(TR, TOK),
            buf(TR, TOK),
            buf(4, TR, TOK),
            buf(4, TOK, TR),
            buf(2, TR, NAR),
            buf(TR, COL),
            buf(2, SR, NAR),
            buf(2, 4 * PACK, NAR),
            buf(2, TR, COL),
            buf(PACK, HALF),
            buf(HALF, PACK),
            buf(3, 2, PACK, HID),
            buf(2, PACK, HID, dtype=F32),
            buf(2, PACK, HID, dtype=F32),
            buf(3, 2, PACK, HID),
            buf(2, PACK, HID),
            buf(2, PACK, HID, dtype=F32),
            buf(2, PACK, HID),
            buf(4 * PACK, HID),
            buf(2 * PACK, HID),
            buf(2 * PACK, COL),
            buf(2 * PACK, COL),
            buf(TR, COL),
            buf(TR, COL),
            buf(4 * PACK, NAR),
            buf(4 * PACK, NAR),
            buf(SR, NAR),
            buf(2, TR, NAR),
            buf(TOK, COL, dtype=F32),
            buf(2, TR, NAR),
            buf(2, SR, NAR),
            buf(2, 4 * PACK, NAR),
            buf(3, PACK, HID),
            buf(PACK, HID, dtype=F32),
            buf(PACK, HID, dtype=F32),
            buf(3, PACK, HID),
            buf(4 * PACK, HID),
            buf(4 * PACK, HID),
            dma((9,)),
            dma((5,)),
            dma((5,)),
            dma((5,)),
            dma((16,)),
            dma((16,)),
            dma((32,)),
            dma((32,)),
        ],
        compiler_params=pltpu.CompilerParams(
            collective_id=0, has_side_effects=True, vmem_limit_bytes=60 << 20
        ),
        cost_estimate=pl.CostEstimate(
            flops=16_000_000_000, bytes_accessed=24_000_000, transcendentals=1_000_000
        ),
        name="distill",
    )(ids.T, gates.T, order.reshape(1, OWNERS), tokens, tg, tu, td, sg, su, sd)
    weight = jax.ShapeDtypeStruct((1, HID, COL), BF)
    return pl.pallas_call(
        finish,
        out_shape=(jax.ShapeDtypeStruct((TOK, COL), F32), weight, weight, weight),
        in_specs=[hbm] * 5,
        out_specs=(hbm,) * 4,
        scratch_shapes=[
            buf(4 * PACK, HID),
            buf(2, 4 * PACK, NAR),
            buf(2, HID, NAR),
            buf(HID, COL),
            buf(HID, COL),
            buf(TOK, COL, dtype=F32),
            dma((11,)),
        ],
        compiler_params=pltpu.CompilerParams(vmem_limit_bytes=60 << 20),
        cost_estimate=pl.CostEstimate(
            flops=1_600_000_000, bytes_accessed=13_000_000, transcendentals=0
        ),
        name="finish",
    )(*parts)


def solution(mesh):
    weights = P("expert", "replica", "group")
    return jax.shard_map(
        shards,
        mesh=mesh,
        in_specs=(P("expert", "group"), P("expert", None), P("expert", None), P()) + (weights,) * 6,
        out_specs=(P("expert", ("group", "replica")), weights, weights, weights),
        check_vma=False,
    )
```
